256 devices in a mesh: replica: 8 (over y, core), fsdp: 32 (over z, x).
Axes of the slice: x: 4, y: 4, z: 8, core: 2. Of those that a mesh axis runs over, the one named last changes fastest.
Arguments:
- local_params: float32 [8, 512, 14336], P('replica', 'fsdp'), may hold values from -6 to 6
- outer_base: float32 [512, 14336], P('fsdp'), may hold values from -6 to 6
- error_memory: float32 [8, 512, 14336], P('replica', 'fsdp'), may hold values from -4 to 4
- momentum: float32 [512, 14336], P('fsdp'), may hold values from -6 to 6
- start_seed: int32 [1], replicated, may hold values from 0 to 65520
Outputs:
- new_error: float32 [8, 512, 14336], P('replica', 'fsdp')
- new_base: float32 [512, 14336], P('fsdp')
- new_momentum: float32 [512, 14336], P('fsdp')
The draws below stay inside these ranges and needn't reach their ends.
All inputs are finite; a program needn't handle non-finite values.
Results may differ from the reference program's by a relative error of at most 0.00007.
Values sent between devices are 32-bit elements; how exact they have to be, the bound alone decides.
A program may use at most 64 MiB of HBM per device.

```python
import jax
import jax.numpy as jnp
from jax import lax

N_COLS = 14336
RANK = 128
ROWS = 512
REPLICAS = 8
N_REPLICA = 8


def raised(drawn, key, source, target, shards_of, factor):
    def block_of(axis_at):
        return (jnp.arange(drawn.shape[axis_at]) // (drawn.shape[axis_at] // shards_of)).reshape((-1,) + (1,) * (drawn.ndim - 1 - axis_at))

    first = jax.random.permutation(key, shards_of)[block_of(target)]
    other_side = (block_of(target) + shards_of // 2) % shards_of
    return jnp.where((block_of(source) == first) | (block_of(source) == other_side), factor * drawn, drawn)


def block_scale(stream_key, shape, shards, smallest, high):
    def one(dim, blocks):
        draws = jax.random.uniform(jax.random.fold_in(jax.random.fold_in(stream_key, 6), dim), (blocks,), jnp.float32, smallest / len(shards), high / len(shards))
        return jnp.repeat(jnp.exp(draws), shape[dim] // blocks).reshape((-1,) + (1,) * (len(shape) - dim - 1))

    factor_of = one(*shards[0])
    for cut in shards[1:]:
        factor_of = factor_of * one(*cut)
    return factor_of


def noise(own_key, extent, deviation, bound, shards=(), kind=jnp.bfloat16):
    loudness = block_scale(own_key, extent, shards, -0.22, 0.18) if shards else 1.0
    values = jax.random.normal(own_key, extent, jnp.float32) * deviation * loudness
    return jnp.minimum(jnp.maximum(values, -bound), bound).astype(kind)


def gaussian_with(own_key, dims, deviation, reach, shards, heavy, dtype=jnp.bfloat16):
    entries = deviation * jax.random.normal(own_key, dims, jnp.float32)
    if shards:
        entries = entries * block_scale(own_key, dims, shards, -0.22, 0.18)
    return jnp.clip(raised(entries, jax.random.fold_in(own_key, 3), *heavy), -reach, reach).astype(dtype)


def setup_inputs(seed: int = 0) -> dict:
    splits = jax.random.split(jax.random.key(seed), 6)
    return {
        "local_params": gaussian_with(splits[0], (REPLICAS, ROWS, N_COLS), 1.0, 6.0, ((0, 8), (1, 32)), (1, 2, 32, 2.75), jnp.float32),
        "outer_base": noise(splits[1], (ROWS, N_COLS), 1.0, 6.0, ((0, 32),), jnp.float32),
        "error_memory": noise(splits[2], (REPLICAS, ROWS, N_COLS), 0.3, 4.0, ((0, 8), (1, 32)), jnp.float32),
        "momentum": noise(splits[3], (ROWS, N_COLS), 0.5, 6.0, ((0, 32),), jnp.float32),
        "start_seed": jax.random.randint(splits[4], (1,), 0, 65521).astype(jnp.int32),
    }


def start_factor(start_seed, col_count, rank_count):
    row_index = lax.broadcasted_iota(jnp.int32, (col_count, rank_count), 0)
    col_index = lax.broadcasted_iota(jnp.int32, (col_count, rank_count), 1)
    mixed = (181 * row_index + 359 * col_index + 1013 * start_seed[0]) % 65521
    hashed = (mixed * (mixed % 32749) + 7 * row_index + 3 * col_index) % 65521
    return (hashed.astype(jnp.float32) / 65521.0 - 0.5) * 3.4641016

def reference(local_params, outer_base, error_memory, momentum, start_seed):
    highest = lax.Precision.HIGHEST
    starting = start_factor(start_seed, N_COLS, RANK)
    corrected = outer_base[None] - local_params + error_memory
    averaged = jnp.sum(corrected, axis=0) / N_REPLICA
    left = jnp.dot(averaged, starting, precision=highest)
    gram_matrix = jnp.dot(left.T, left, precision=highest)
    chol_factor = jnp.linalg.cholesky(gram_matrix)
    ortho = jax.scipy.linalg.solve_triangular(chol_factor, left.T, lower=True).T
    right = jnp.dot(averaged.T, ortho, precision=highest)
    approx = jnp.dot(ortho, right.T, precision=highest)
    new_error = corrected - approx[None]
    new_momentum = 0.9 * momentum + approx
    new_base = outer_base - 0.7 * (approx + 0.9 * new_momentum)
    return (new_error, new_base, new_momentum)
```

```python
import functools

import jax
import jax.numpy as jnp
from jax import lax
from jax.experimental import pallas as pl
from jax.experimental.pallas import tpu as pltpu
from jax.sharding import PartitionSpec as P

RANK = 128
LANES = 128
SUBS = 8
HIGHEST = lax.Precision.HIGHEST
MESH = pl.DeviceIdType.MESH


def owner_of(tile, tiles, fsdp):
    return tile if tiles == fsdp else tile + 1 + tile // 8


def tile_of(f, tiles, fsdp):
    if tiles == fsdp:
        return f >= 0, f
    tile = f - 1 - f // 9
    return jnp.logical_and(lax.rem(f, 9) != 0, tile < tiles), tile


def write_start_factor(seed, first_row, out_ref):
    k = lax.broadcasted_iota(jnp.int32, (SUBS, LANES), 1)
    j = lax.broadcasted_iota(jnp.int32, (SUBS, LANES), 0) + first_row
    mixed = lax.rem(181 * j + 359 * k + 1013 * seed, 65521)
    added = 7 * j + 3 * k

    def rows(i, carry):
        mixed, added = carry
        low = jnp.where(mixed >= 65498, mixed - 65498, jnp.where(mixed >= 32749, mixed - 32749, mixed))
        value = mixed * low + added
        quotient = (value.astype(jnp.float32) * (1.0 / 65521.0)).astype(jnp.int32)
        rest = value - quotient * 65521
        rest = jnp.where(rest < 0, rest + 65521, rest)
        rest = jnp.where(rest >= 65521, rest - 65521, rest)
        drawn = (rest.astype(jnp.float32) * (1.0 / 65521.0) - 0.5) * 3.4641016
        out_ref[pl.ds(pl.multiple_of(i * SUBS, SUBS), SUBS), :] = drawn
        mixed = mixed + 181 * SUBS
        return jnp.where(mixed >= 65521, mixed - 65521, mixed), added + 7 * SUBS

    lax.fori_loop(0, out_ref.shape[0] // SUBS, rows, (mixed, added), unroll=8)


def solve(mg, mw):
    sub = lax.broadcasted_iota(jnp.int32, (SUBS, LANES), 0)

    def col(x, lane):
        return jnp.broadcast_to(x[:, lane : lane + 1], (SUBS, LANES))

    def row(x, i):
        return jnp.broadcast_to(x[i : i + 1, :], (SUBS, LANES))

    panels = RANK // SUBS
    for p in range(panels):
        pg, pw = mg[p], mw[p]
        cols = [col(pg, SUBS * p + j) for j in range(SUBS)]
        for i in range(SUBS):
            scale = 1.0 / row(cols[i], i)
            here = sub == i
            by = cols[i]

            def step(x):
                pivot_row = row(x, i) * scale
                return jnp.where(here, pivot_row, x - by * pivot_row)

            pg, pw = step(pg), step(pw)
            for j in range(i + 1, SUBS):
                cols[j] = step(cols[j])
        g_rows = [row(pg, j) for j in range(SUBS)]
        w_rows = [row(pw, j) for j in range(SUBS)]
        for q in [(p + 1 + k) % panels for k in range(panels - 1)]:
            a, b = mg[q], mw[q]
            by = [col(a, SUBS * p + j) for j in range(SUBS)]

            def taken(rows):
                t = [by[j] * rows[j] for j in range(SUBS)]
                return ((t[0] + t[1]) + (t[2] + t[3])) + ((t[4] + t[5]) + (t[6] + t[7]))

            if p < panels - 1:
                mg[q] = a - taken(g_rows)
            mw[q] = b - taken(w_rows)
        if p < panels - 1:
            mg[p] = pg
        mw[p] = pw


def wait_for(ref, sem):
    pltpu.make_async_copy(ref, ref, sem).wait()


def kernel(
    replicas, fsdp, tiles,
    seed_ref, lp_hbm, base_hbm, err_hbm, out_hbm,
    cor, basev, errv, sib, rs, blk, start, parts, left, at, ap, apx, mg, mw,
    load_sem, p1_send, p1_recv, p2_send, p2_recv, p3_sem, p4_sem, px_sem, p5_sem, p7_sem,
    p8_send, p8_recv, p9_send, p9_recv, out_sem,
):
    chips = replicas // 2
    width = tiles * LANES
    r = lax.axis_index("replica")
    f = lax.axis_index("fsdp")
    c = lax.rem(r, 2)
    y = r // 2
    sibling = {"replica": 2 * y + 1 - c, "fsdp": f}
    shifts = [1, 3, 2, 0] if chips == 4 else [*range(1, chips), 0]

    def cols(block):
        return pl.ds(pl.multiple_of(block * width, LANES), width)

    def chip(shift):
        return lax.rem(y + shift, chips)

    def send(src, dst, s, d, to):
        pltpu.make_async_remote_copy(
            src_ref=src, dst_ref=dst, send_sem=s, recv_sem=d, device_id=to, device_id_type=MESH
        ).start()

    order = [2 * chip(s) + 1 - c for s in shifts] + [2 * chip(s) + c for s in shifts]
    loads = []
    for n, block in enumerate(order):
        at_cols = cols(block)
        three = [
            pltpu.make_async_copy(src.at[:, :, at_cols], dst.at[:, :, at_cols], load_sem.at[n, i])
            for i, (src, dst) in enumerate(((lp_hbm, cor), (base_hbm, basev), (err_hbm, errv)))
        ]
        for copy in three:
            copy.start()
        loads.append(three)

    barrier = pltpu.get_barrier_semaphore()
    for k in range(1, replicas):
        pl.semaphore_signal(
            barrier, inc=1, device_id={"replica": lax.rem(r + k, replicas), "fsdp": f}, device_id_type=MESH
        )

    def greet(k, _):
        pl.semaphore_signal(
            barrier, inc=1, device_id={"replica": r, "fsdp": lax.rem(f + k, fsdp)}, device_id_type=MESH
        )
        return 0

    lax.fori_loop(1, fsdp, greet, 0)

    write_start_factor(seed_ref[0], r * width, start)

    def correct(n):
        for copy in loads[n]:
            copy.wait()
        at_cols = cols(order[n])
        cor[:, :, at_cols] = basev[:, :, at_cols] - cor[:, :, at_cols] + errv[:, :, at_cols]

    correct(0)
    pl.semaphore_wait(barrier, replicas - 1 + fsdp - 1)

    for k in range(chips):
        if k > 0:
            correct(k)
        send(cor.at[:, :, cols(order[k])], sib.at[k], p1_send.at[k], p1_recv.at[k], sibling)
    for k, shift in enumerate(shifts):
        correct(chips + k)
        wait_for(sib.at[k], p1_recv.at[k])
        sib[k] = sib[k] + cor[:, :, cols(order[chips + k])]
        if shift:
            send(sib.at[k], rs.at[k], p2_send.at[k], p2_recv.at[k], {"replica": 2 * chip(shift) + c, "fsdp": f})
    total = sib[chips - 1]
    for k in range(chips - 1):
        wait_for(rs.at[k], p2_recv.at[k])
        total = total + rs[k]
    blk[...] = total * (1.0 / replicas)

    rows = 2 * blk.shape[1]
    parts[r] = jnp.dot(
        blk[...].reshape(rows, width), start[...], precision=HIGHEST, preferred_element_type=jnp.float32
    ).reshape(parts.shape[1:])
    for k in range(1, replicas):
        send(parts.at[r], parts.at[r], p3_sem.at[0], p3_sem.at[1], {"replica": lax.rem(r + k, replicas), "fsdp": f})

    has_tile, my_tile = tile_of(f, 2 * tiles, fsdp)
    owner = jnp.logical_and(has_tile, lax.rem(my_tile, 2) == c)
    my_tile = my_tile // 2
    for t in range(tiles):
        to = owner_of(2 * t + c, 2 * tiles, fsdp)
        tile = blk.at[:, :, t * LANES : (t + 1) * LANES]

        @pl.when(to != f)
        def _():
            send(tile, at.at[:, f], p5_sem.at[0], p5_sem.at[1], {"replica": r, "fsdp": to})

        @pl.when(to == f)
        def _():
            at[:, f] = tile[...]

    wait_for(parts.at[pl.ds(0, replicas - 1)], p3_sem.at[1])
    mine = parts[0, c]
    for k in range(1, replicas):
        mine = mine + parts[k, c]
    left[c, f] = mine

    def spread(k, _):
        send(left.at[c, f], left.at[c, f], p4_sem.at[0], p4_sem.at[1], {"replica": r, "fsdp": lax.rem(f + k, fsdp)})
        return 0

    lax.fori_loop(1, fsdp, spread, 0)
    wait_for(left.at[c, pl.ds(0, fsdp - 1)], p4_sem.at[1])
    send(left.at[c], left.at[c], px_sem.at[0], px_sem.at[1], sibling)
    wait_for(left.at[1 - c], px_sem.at[1])

    my_cols = pl.ds(pl.multiple_of((r * tiles + my_tile) * LANES, LANES), LANES)

    @pl.when(owner)
    def _():
        wait_for(at.at[:, pl.ds(0, fsdp - 1)], p5_sem.at[1])
        whole = left[...].reshape(fsdp * rows, RANK)
        against = (((0,), (0,)), ((), ()))
        mg[...] = lax.dot_general(
            whole, whole, against, precision=HIGHEST, preferred_element_type=jnp.float32
        ).reshape(mg.shape)
        mw[...] = lax.dot_general(
            whole, at[...].reshape(fsdp * rows, LANES), against, precision=HIGHEST, preferred_element_type=jnp.float32
        ).reshape(mw.shape)
        solve(mg, mw)
        ap[...] = jnp.dot(
            whole, mw[...].reshape(RANK, LANES), precision=HIGHEST, preferred_element_type=jnp.float32
        ).reshape(ap.shape)

        def give(k, _):
            to = lax.rem(f + k, fsdp)
            send(ap.at[:, to], apx.at[:, :, my_cols], p7_sem.at[0], p7_sem.at[1], {"replica": r, "fsdp": to})
            return 0

        lax.fori_loop(1, fsdp, give, 0)
        apx[:, :, my_cols] = ap[:, f]
        wait_for(at.at[:, pl.ds(0, tiles - 1)], p7_sem.at[1])

    @pl.when(jnp.logical_not(owner))
    def _():
        wait_for(at.at[:, pl.ds(0, tiles)], p7_sem.at[1])

    def place(block):
        return apx.at[:, :, cols(block)]

    for k, shift in enumerate(shifts[:-1]):
        send(place(r), place(r), p8_send.at[k], p8_recv.at[k], {"replica": 2 * chip(shift) + c, "fsdp": f})
    send(place(r), place(r), p9_send.at[chips - 1], p9_recv.at[chips - 1], sibling)
    outs = []

    def write_out(block):
        copy = pltpu.make_async_copy(place(block), out_hbm.at[:, :, cols(block)], out_sem.at[len(outs)])
        copy.start()
        outs.append(copy)

    write_out(r)
    for k, shift in enumerate(shifts[:-1]):
        block = 2 * chip(chips - shift) + c
        wait_for(place(block), p8_recv.at[k])
        send(place(block), place(block), p9_send.at[k], p9_recv.at[k], sibling)
        write_out(block)
    for k, shift in [(chips - 1, 0), *enumerate(shifts[:-1])]:
        block = 2 * chip(chips - shift) + 1 - c
        wait_for(place(block), p9_recv.at[k])
        write_out(block)

    for k in range(chips):
        wait_for(sib.at[k], p1_send.at[k])
        wait_for(sib.at[k], p9_send.at[k])
        if k < chips - 1:
            wait_for(sib.at[k], p2_send.at[k])
            wait_for(sib.at[k], p8_send.at[k])
    wait_for(parts.at[pl.ds(0, replicas - 1)], p3_sem.at[0])
    wait_for(left.at[c, pl.ds(0, fsdp - 1)], p4_sem.at[0])
    wait_for(left.at[c], px_sem.at[0])

    own_tile_here = jnp.logical_and(owner, my_tile < tiles)

    @pl.when(own_tile_here)
    def _():
        wait_for(at.at[:, pl.ds(0, tiles - 1)], p5_sem.at[0])
        wait_for(ap.at[:, pl.ds(0, fsdp - 1)], p7_sem.at[0])

    @pl.when(jnp.logical_not(own_tile_here))
    def _():
        wait_for(at.at[:, pl.ds(0, tiles)], p5_sem.at[0])

    for copy in outs:
        copy.wait()


def approximate(local_params, outer_base, error_memory, start_seed):
    replicas, fsdp = lax.axis_size("replica"), lax.axis_size("fsdp")
    rows, columns = outer_base.shape
    half = rows // 2
    tiles = columns // replicas // LANES
    width = tiles * LANES
    chips = replicas // 2
    f32 = jnp.float32
    whole = (2, half, columns)
    dma = pltpu.SemaphoreType.DMA
    anywhere = pl.BlockSpec(memory_space=pl.ANY)
    found = pl.pallas_call(
        functools.partial(kernel, replicas, fsdp, tiles),
        out_shape=jax.ShapeDtypeStruct(whole, f32),
        in_specs=[pl.BlockSpec(memory_space=pltpu.SMEM), anywhere, anywhere, anywhere],
        out_specs=anywhere,
        scratch_shapes=[
            pltpu.VMEM(whole, f32),
            pltpu.VMEM(whole, f32),
            pltpu.VMEM(whole, f32),
            pltpu.VMEM((chips, 2, half, width), f32),
            pltpu.VMEM((chips - 1, 2, half, width), f32),
            pltpu.VMEM((2, half, width), f32),
            pltpu.VMEM((width, RANK), f32),
            pltpu.VMEM((replicas, 2, half, RANK), f32),
            pltpu.VMEM((2, fsdp, half, RANK), f32),
            pltpu.VMEM((2, fsdp, half, LANES), f32),
            pltpu.VMEM((2, fsdp, half, LANES), f32),
            pltpu.VMEM(whole, f32),
            pltpu.VMEM((RANK // SUBS, SUBS, RANK), f32),
            pltpu.VMEM((RANK // SUBS, SUBS, LANES), f32),
            dma((replicas, 3)),
            dma((chips,)),
            dma((chips,)),
            dma((chips,)),
            dma((chips,)),
            dma((2,)),
            dma((2,)),
            dma((2,)),
            dma((2,)),
            dma((2,)),
            dma((chips,)),
            dma((chips,)),
            dma((chips,)),
            dma((chips,)),
            dma((replicas,)),
        ],
        compiler_params=pltpu.CompilerParams(
            collective_id=0, has_side_effects=True, vmem_limit_bytes=48 * 1024 * 1024
        ),
        cost_estimate=pl.CostEstimate(flops=10**9, bytes_accessed=4 * 10**6, transcendentals=0),
        name="approximate",
    )(
        start_seed,
        local_params.reshape(whole),
        outer_base.reshape(whole),
        error_memory.reshape(whole),
    )
    return found.reshape(rows, columns)


def on_device(local_params, outer_base, error_memory, momentum, start_seed):
    approx = approximate(local_params[0], outer_base, error_memory[0], start_seed)
    corrected = outer_base - local_params[0] + error_memory[0]
    new_error = (corrected - approx)[None]
    new_momentum = 0.9 * momentum + approx
    new_base = outer_base - 0.7 * (approx + 0.9 * new_momentum)
    return (new_error, new_base, new_momentum)


def solution(mesh):
    placed = (
        P("replica", "fsdp", None),
        P("fsdp", None),
        P("replica", "fsdp", None),
        P("fsdp", None),
        P(),
    )
    return jax.shard_map(
        on_device,
        mesh=mesh,
        in_specs=placed,
        out_specs=(P("replica", "fsdp", None), P("fsdp", None), P("fsdp", None)),
        check_vma=False,
    )
```

```python
import functools

import jax
import jax.numpy as jnp
from jax import lax
from jax.experimental import pallas as pl
from jax.experimental.pallas import tpu as pltpu
from jax.sharding import PartitionSpec as P

RANK = 128
LANES = 128
SUBS = 8
HIGHEST = lax.Precision.HIGHEST
MESH = pl.DeviceIdType.MESH


def owner_of(tile, tiles, fsdp):
    return tile if tiles == fsdp else tile + 1 + tile // 8


def tile_of(f, tiles, fsdp):
    if tiles == fsdp:
        return f >= 0, f
    tile = f - 1 - f // 9
    return jnp.logical_and(lax.rem(f, 9) != 0, tile < tiles), tile


def write_start_factor(seed, first_row, out_ref):
    k = lax.broadcasted_iota(jnp.int32, (SUBS, LANES), 1)
    j = lax.broadcasted_iota(jnp.int32, (SUBS, LANES), 0) + first_row
    mixed = lax.rem(181 * j + 359 * k + 1013 * seed, 65521)
    added = 7 * j + 3 * k

    def rows(i, carry):
        mixed, added = carry
        low = jnp.where(mixed >= 65498, mixed - 65498, jnp.where(mixed >= 32749, mixed - 32749, mixed))
        value = mixed * low + added
        quotient = (value.astype(jnp.float32) * (1.0 / 65521.0)).astype(jnp.int32)
        rest = value - quotient * 65521
        rest = jnp.where(rest < 0, rest + 65521, rest)
        rest = jnp.where(rest >= 65521, rest - 65521, rest)
        drawn = (rest.astype(jnp.float32) * (1.0 / 65521.0) - 0.5) * 3.4641016
        out_ref[pl.ds(pl.multiple_of(i * SUBS, SUBS), SUBS), :] = drawn
        mixed = mixed + 181 * SUBS
        return jnp.where(mixed >= 65521, mixed - 65521, mixed), added + 7 * SUBS

    lax.fori_loop(0, out_ref.shape[0] // SUBS, rows, (mixed, added), unroll=8)


def solve(mg, mw):
    sub = lax.broadcasted_iota(jnp.int32, (SUBS, LANES), 0)

    def col(x, lane):
        return jnp.broadcast_to(x[:, lane : lane + 1], (SUBS, LANES))

    def row(x, i):
        return jnp.broadcast_to(x[i : i + 1, :], (SUBS, LANES))

    panels = RANK // SUBS
    for p in range(panels):
        pg, pw = mg[p], mw[p]
        cols = [col(pg, SUBS * p + j) for j in range(SUBS)]
        for i in range(SUBS):
            scale = 1.0 / row(cols[i], i)
            here = sub == i
            by = cols[i]

            def step(x):
                pivot_row = row(x, i) * scale
                return jnp.where(here, pivot_row, x - by * pivot_row)

            pg, pw = step(pg), step(pw)
            for j in range(i + 1, SUBS):
                cols[j] = step(cols[j])
        g_rows = [row(pg, j) for j in range(SUBS)]
        w_rows = [row(pw, j) for j in range(SUBS)]
        for q in [(p + 1 + k) % panels for k in range(panels - 1)]:
            a, b = mg[q], mw[q]
            by = [col(a, SUBS * p + j) for j in range(SUBS)]

            def taken(rows):
                t = [by[j] * rows[j] for j in range(SUBS)]
                return ((t[0] + t[1]) + (t[2] + t[3])) + ((t[4] + t[5]) + (t[6] + t[7]))

            if p < panels - 1:
                mg[q] = a - taken(g_rows)
            mw[q] = b - taken(w_rows)
        if p < panels - 1:
            mg[p] = pg
        mw[p] = pw


def wait_for(ref, sem):
    if 0 in ref.shape:
        return
    pltpu.make_async_copy(ref, ref, sem).wait()


def kernel(
    replicas, fsdp, tiles,
    seed_ref, lp_hbm, base_hbm, err_hbm, apx, cor, basev,
    errv, sib, relay, rs, blk, start, part, parts, mine, left, at, ap, mg, mw,
    load_sem, p1_send, p1_recv, p2_send, p2_recv, p3_sem, p4_sem, p5_sem, p7_send, p7_recv,
    p8_send, p8_recv, p9_send, p9_recv,
):
    chips = replicas // 2
    width = tiles * LANES
    half = blk.shape[1]
    r = lax.axis_index("replica")
    f = lax.axis_index("fsdp")
    c = lax.rem(r, 2)
    y = r // 2
    sibling = {"replica": 2 * y + 1 - c, "fsdp": f}
    shifts = [2, 1, 3, 0]

    def cols(block):
        return pl.ds(pl.multiple_of(block * width, LANES), width)

    def chip(shift):
        return lax.rem(y + shift, chips)

    def along_y(shift):
        return {"replica": 2 * chip(shift) + c, "fsdp": f}

    def send(src, dst, s, d, to):
        pltpu.make_async_remote_copy(
            src_ref=src, dst_ref=dst, send_sem=s, recv_sem=d, device_id=to, device_id_type=MESH
        ).start()

    drains = []

    def finish():
        for condition, ref, sem in drains:
            if condition is None:
                wait_for(ref, sem)
            else:

                @pl.when(condition)
                def _():
                    wait_for(ref, sem)

    order = [2 * chip(s) + 1 - c for s in shifts] + [2 * chip(s) + c for s in shifts]
    loads = []
    for n, block in enumerate(order):
        at_cols = cols(block)
        three = [
            pltpu.make_async_copy(src.at[:, :, at_cols], dst.at[:, :, at_cols], load_sem.at[n, i])
            for i, (src, dst) in enumerate(((lp_hbm, cor), (base_hbm, basev), (err_hbm, errv)))
        ]
        for copy in three:
            copy.start()
        loads.append(three)

    barrier = pltpu.get_barrier_semaphore()
    for k in range(1, replicas):
        pl.semaphore_signal(
            barrier, inc=1, device_id={"replica": lax.rem(r + k, replicas), "fsdp": f}, device_id_type=MESH
        )
    def greet(k, _):
        for core in range(2):
            pl.semaphore_signal(
                barrier, inc=1, device_id={"replica": 2 * y + core, "fsdp": lax.rem(f + k, fsdp)}, device_id_type=MESH
            )
        return 0

    lax.fori_loop(1, fsdp, greet, 0)

    def correct(n):
        for copy in loads[n]:
            copy.wait()
        at_cols = cols(order[n])
        cor[:, :, at_cols] = basev[:, :, at_cols] - cor[:, :, at_cols] + errv[:, :, at_cols]

    correct(0)
    pl.semaphore_wait(barrier, replicas - 1 + 2 * (fsdp - 1))

    for k in range(chips):
        if k > 0:
            correct(k)
        send(cor.at[:, :, cols(order[k])], sib.at[k], p1_send.at[k], p1_recv.at[k], sibling)
        drains.append((None, sib.at[k], p1_send.at[k]))

    def paired(k):
        correct(chips + k)
        wait_for(sib.at[k], p1_recv.at[k])
        sib[k] = sib[k] + cor[:, :, cols(order[chips + k])]

    def hop(n, src, dst, shift):
        send(src, dst, p2_send.at[n], p2_recv.at[n], along_y(shift))
        drains.append((None, src, p2_send.at[n]))

    paired(0)
    hop(0, sib.at[0, 0], relay.at[0], 1)
    hop(1, sib.at[0, 1], relay.at[1], 3)
    paired(1)
    hop(2, sib.at[1, 1], rs.at[0, 1], 1)
    paired(2)
    hop(3, sib.at[2, 0], rs.at[1, 0], 3)
    paired(3)
    wait_for(relay.at[0], p2_recv.at[0])
    relay[0] = relay[0] + sib[1, 0]
    hop(4, relay.at[0], rs.at[0, 0], 1)
    wait_for(relay.at[1], p2_recv.at[1])
    relay[1] = relay[1] + sib[2, 1]
    hop(5, relay.at[1], rs.at[1, 1], 3)
    write_start_factor(seed_ref[0], r * width, start)
    for n, (a, b) in zip((2, 3, 4, 5), ((0, 1), (1, 0), (0, 0), (1, 1)), strict=True):
        wait_for(rs.at[a, b], p2_recv.at[n])
    blk[...] = (sib[3] + rs[0] + rs[1]) * (1.0 / replicas)

    rows = 2 * half
    part[...] = jnp.dot(
        blk[...].reshape(rows, width), start[...], precision=HIGHEST, preferred_element_type=jnp.float32
    ).reshape(part.shape)
    parts[r] = part[c]
    for k in range(1, replicas):
        to = lax.rem(r + k, replicas)
        send(part.at[lax.rem(to, 2)], parts.at[r], p3_sem.at[0], p3_sem.at[1], {"replica": to, "fsdp": f})
    drains.append((None, parts.at[pl.ds(0, replicas - 1)], p3_sem.at[0]))

    has_tile, my_tile = tile_of(f, 2 * tiles, fsdp)
    owner = jnp.logical_and(has_tile, lax.rem(my_tile, 2) == c)
    other = jnp.logical_not(owner)
    my_tile = my_tile // 2
    for t in range(tiles):
        to = owner_of(2 * t + c, 2 * tiles, fsdp)
        tile = blk.at[:, :, t * LANES : (t + 1) * LANES]

        @pl.when(to != f)
        def _():
            send(tile, at.at[:, f], p5_sem.at[0], p5_sem.at[1], {"replica": r, "fsdp": to})

        @pl.when(to == f)
        def _():
            at[:, f] = tile[...]

    drains.append((owner, at.at[:, pl.ds(0, tiles - 1)], p5_sem.at[0]))
    drains.append((other, at.at[:, pl.ds(0, tiles)], p5_sem.at[0]))

    wait_for(parts.at[pl.ds(0, replicas - 1)], p3_sem.at[1])
    total = parts[0]
    for k in range(1, replicas):
        total = total + parts[k]
    mine[...] = total

    def spread(k, _):
        there = lax.rem(f + k, fsdp)
        has, tile = tile_of(there, 2 * tiles, fsdp)
        core = lax.rem(tile, 2)

        @pl.when(jnp.logical_and(has, jnp.logical_or(k > 0, core != c)))
        def _():
            send(mine, left.at[c * fsdp + f], p4_sem.at[0], p4_sem.at[1], {"replica": 2 * y + core, "fsdp": there})

        return 0

    lax.fori_loop(0, fsdp, spread, 0)
    drains.append((owner, left.at[pl.ds(0, 2 * tiles - 1)], p4_sem.at[0]))
    drains.append((other, left.at[pl.ds(0, 2 * tiles)], p4_sem.at[0]))

    my_cols = pl.ds(pl.multiple_of((r * tiles + my_tile) * LANES, LANES), LANES)

    @pl.when(owner)
    def _():
        left[c * fsdp + f] = total
        wait_for(at.at[:, pl.ds(0, fsdp - 1)], p5_sem.at[1])
        wait_for(left.at[pl.ds(0, 2 * fsdp - 1)], p4_sem.at[1])
        whole = left[...].reshape(fsdp * rows, RANK)
        against = (((0,), (0,)), ((), ()))
        mg[...] = lax.dot_general(
            whole, whole, against, precision=HIGHEST, preferred_element_type=jnp.float32
        ).reshape(mg.shape)
        mw[...] = lax.dot_general(
            whole, at[...].reshape(fsdp * rows, LANES), against, precision=HIGHEST, preferred_element_type=jnp.float32
        ).reshape(mw.shape)
        solve(mg, mw)
        for h in range(2):
            ap[h] = jnp.dot(
                left[pl.ds(h * fsdp, fsdp)].reshape(fsdp * half, RANK),
                mw[...].reshape(RANK, LANES),
                precision=HIGHEST,
                preferred_element_type=jnp.float32,
            ).reshape(ap.shape[1:])

            def give(k, _):
                to = lax.rem(f + k, fsdp)
                send(ap.at[h, to], apx.at[h, :, my_cols], p7_send.at[h], p7_recv.at[h], {"replica": r, "fsdp": to})
                return 0

            lax.fori_loop(1, fsdp, give, 0)
            apx[h, :, my_cols] = ap[h, f]

    def place(h, block):
        return apx.at[h, :, cols(block)]

    for h in range(2):
        drains.append((owner, ap.at[0, pl.ds(0, fsdp - 1)], p7_send.at[h]))

        @pl.when(owner)
        def _():
            wait_for(ap.at[0, pl.ds(0, tiles - 1)], p7_recv.at[h])

        @pl.when(other)
        def _():
            wait_for(ap.at[0, pl.ds(0, tiles)], p7_recv.at[h])

        for k, shift in enumerate(shifts):
            if shift:
                send(place(h, r), place(h, r), p8_send.at[h, k], p8_recv.at[h, k], along_y(shift))
                drains.append((None, blk.at[0], p8_send.at[h, k]))
            else:
                send(place(h, r), place(h, r), p9_send.at[h, k], p9_recv.at[h, k], sibling)
            drains.append((None, blk.at[0], p9_send.at[h, k]))

    for h in range(2):
        for k in (1, 2, 0):
            block = 2 * chip(chips - shifts[k]) + c
            wait_for(place(h, block), p8_recv.at[h, k])
            send(place(h, block), place(h, block), p9_send.at[h, k], p9_recv.at[h, k], sibling)
    for h in range(2):
        for k in range(chips):
            wait_for(blk.at[0], p9_recv.at[h, k])
    finish()


def approximate(local_params, outer_base, error_memory, start_seed):
    replicas, fsdp = lax.axis_size("replica"), lax.axis_size("fsdp")
    rows, columns = outer_base.shape
    half = rows // 2
    tiles = columns // replicas // LANES
    width = tiles * LANES
    chips = replicas // 2
    f32 = jnp.float32
    whole = (2, half, columns)
    dma = pltpu.SemaphoreType.DMA
    in_hbm = pl.BlockSpec(memory_space=pltpu.HBM)
    found = pl.pallas_call(
        functools.partial(kernel, replicas, fsdp, tiles),
        out_shape=[pltpu.VMEM(whole, f32)] * 3,
        in_specs=[pl.BlockSpec(memory_space=pltpu.SMEM), in_hbm, in_hbm, in_hbm],
        out_specs=[pl.BlockSpec(memory_space=pltpu.VMEM)] * 3,
        scratch_shapes=[
            pltpu.VMEM(whole, f32),
            pltpu.VMEM((chips, 2, half, width), f32),
            pltpu.VMEM((2, half, width), f32),
            pltpu.VMEM((2, 2, half, width), f32),
            pltpu.VMEM((2, half, width), f32),
            pltpu.VMEM((width, RANK), f32),
            pltpu.VMEM((2, half, RANK), f32),
            pltpu.VMEM((replicas, half, RANK), f32),
            pltpu.VMEM((half, RANK), f32),
            pltpu.VMEM((2 * fsdp, half, RANK), f32),
            pltpu.VMEM((2, fsdp, half, LANES), f32),
            pltpu.VMEM((2, fsdp, half, LANES), f32),
            pltpu.VMEM((RANK // SUBS, SUBS, RANK), f32),
            pltpu.VMEM((RANK // SUBS, SUBS, LANES), f32),
            dma((replicas, 3)),
            dma((chips,)),
            dma((chips,)),
            dma((6,)),
            dma((6,)),
            dma((2,)),
            dma((2,)),
            dma((2,)),
            dma((2,)),
            dma((2,)),
            dma((2, chips)),
            dma((2, chips)),
            dma((2, chips)),
            dma((2, chips)),
        ],
        compiler_params=pltpu.CompilerParams(
            collective_id=0, has_side_effects=True, vmem_limit_bytes=61 * 1024 * 1024
        ),
        cost_estimate=pl.CostEstimate(flops=10**9, bytes_accessed=4 * 10**6, transcendentals=0),
        name="approximate",
    )(
        start_seed,
        local_params.reshape(whole),
        outer_base.reshape(whole),
        error_memory.reshape(whole),
    )
    return [x.reshape(rows, columns) for x in found]


def on_device(local_params, outer_base, error_memory, momentum, start_seed):
    approx, corrected, base = approximate(local_params[0], outer_base, error_memory[0], start_seed)
    new_error = (corrected - approx)[None]
    new_momentum = 0.9 * momentum + approx
    new_base = base - 0.7 * (approx + 0.9 * new_momentum)
    return (new_error, new_base, new_momentum)


def solution(mesh):
    placed = (
        P("replica", "fsdp", None),
        P("fsdp", None),
        P("replica", "fsdp", None),
        P("fsdp", None),
        P(),
    )
    return jax.shard_map(
        on_device,
        mesh=mesh,
        in_specs=placed,
        out_specs=(P("replica", "fsdp", None), P("fsdp", None), P("fsdp", None)),
        check_vma=False,
    )
```

```python
import functools

import jax
import jax.numpy as jnp
from jax import lax
from jax.experimental import pallas as pl
from jax.experimental.pallas import tpu as pltpu
from jax.sharding import PartitionSpec as P

RANK = 128
LANES = 128
SUBS = 8
HIGHEST = lax.Precision.HIGHEST
MESH = pl.DeviceIdType.MESH


def owner_of(tile, tiles, fsdp):
    return tile if tiles == fsdp else tile + 1 + tile // 8


def tile_of(f, tiles, fsdp):
    if tiles == fsdp:
        return f >= 0, f
    tile = f - 1 - f // 9
    return jnp.logical_and(lax.rem(f, 9) != 0, tile < tiles), tile


def write_start_factor(seed, first_row, out_ref):
    two = 2 * SUBS
    k = lax.broadcasted_iota(jnp.int32, (two, LANES), 1)
    j = lax.broadcasted_iota(jnp.int32, (two, LANES), 0) + first_row
    mixed = lax.rem(181 * j + 359 * k + 1013 * seed, 65521)
    added = 7 * j + 3 * k

    def rows(i, carry):
        mixed, added = carry
        low = jnp.where(mixed >= 65498, mixed - 65498, jnp.where(mixed >= 32749, mixed - 32749, mixed))
        value = mixed * low + added
        quotient = (value.astype(jnp.float32) * ((1.0 - 2.0**-21) / 65521.0)).astype(jnp.int32)
        rest = value - quotient * 65521
        rest = jnp.where(rest >= 65521, rest - 65521, rest)
        odd = 2 * rest - 65521
        high = (odd + 256) >> 9
        here = pl.ds(pl.multiple_of(i * two, two), two)
        out_ref[here, :LANES] = high.astype(jnp.float32).astype(jnp.bfloat16)
        out_ref[here, LANES:] = (odd - 512 * high).astype(jnp.float32).astype(jnp.bfloat16)
        mixed = mixed + 181 * two
        return jnp.where(mixed >= 65521, mixed - 65521, mixed), added + 7 * two

    lax.fori_loop(0, out_ref.shape[0] // two, rows, (mixed, added), unroll=8)


def times_start_factor(x, start):
    parts, rest = [], x
    for _ in range(3):
        parts.append(rest.astype(jnp.bfloat16))
        rest = rest - parts[-1].astype(jnp.float32)
    both = jnp.dot(jnp.concatenate(parts, axis=0), start, preferred_element_type=jnp.float32)
    wide = 512.0 * both[:, :LANES] + both[:, LANES:]
    n = x.shape[0]
    return (wide[2 * n :] + wide[n : 2 * n]) + wide[:n]


def invert(m):
    sub = lax.broadcasted_iota(jnp.int32, (SUBS, LANES), 0)
    lane = lax.broadcasted_iota(jnp.int32, (SUBS, LANES), 1)

    def col(x, at):
        return jnp.broadcast_to(x[:, at : at + 1], (SUBS, LANES))

    def row(x, i):
        return jnp.broadcast_to(x[i : i + 1, :], (SUBS, LANES))

    panels = RANK // SUBS
    for p in range(panels):
        first = SUBS * p
        x = m[p]
        cols = [col(x, first + j) for j in range(SUBS)]
        inside = jnp.logical_and(lane >= first, lane < first + SUBS)
        x = jnp.where(inside, jnp.where(lane - first == sub, 1.0, 0.0), x)
        for i in range(SUBS):
            scale = 1.0 / row(cols[i], i)
            here = sub == i
            by = cols[i]

            def step(x):
                pivot_row = row(x, i) * scale
                return jnp.where(here, pivot_row, x - by * pivot_row)

            x = step(x)
            for j in range(i + 1, SUBS):
                cols[j] = step(cols[j])
        rows = [row(x, j) for j in range(SUBS)]
        for q in [(p + 1 + k) % panels for k in range(panels - 1)]:
            a = m[q]
            t = [col(a, first + j) * rows[j] for j in range(SUBS)]
            taken = ((t[0] + t[1]) + (t[2] + t[3])) + ((t[4] + t[5]) + (t[6] + t[7]))
            m[q] = jnp.where(inside, 0.0, a) - taken
        m[p] = x


def along_x(fsdp):
    return 4 if fsdp % 8 == 0 else 2


def wait_for(ref, sem):
    if 0 in ref.shape:
        return
    pltpu.make_async_copy(ref, ref, sem).wait()


def kernel(
    replicas, fsdp, tiles,
    seed_ref, lp_hbm, base_hbm, err_hbm, mom_hbm, cor, basev, momv,
    errv, sib, relay, rs, blk, start, part, parts, line, left, at, ap, apx, mg,
    load_sem, mom_sem, p1_send, p1_recv, p2_send, p2_recv, p3_sem, pz_sem, px_send, px_recv, p5_sem, p7_send, p7_recv,
    p8_send, p8_recv, p9_send, p9_recv,
):
    chips = replicas // 2
    width = tiles * LANES
    half = blk.shape[2]
    rows = 2 * half
    r = lax.axis_index("replica")
    f = lax.axis_index("fsdp")
    c = lax.rem(r, 2)
    y = r // 2
    nx = along_x(fsdp)
    nz = fsdp // nx
    z, x = f // nx, lax.rem(f, nx)
    sibling = {"replica": 2 * y + 1 - c, "fsdp": f}
    shifts = [2, 1, 3, 0]

    def cols(block):
        return pl.ds(pl.multiple_of(block * width, LANES), width)

    def chip(shift):
        return lax.rem(y + shift, chips)

    def along_y(shift):
        return {"replica": 2 * chip(shift) + c, "fsdp": f}

    def send(src, dst, s, d, to):
        pltpu.make_async_remote_copy(
            src_ref=src, dst_ref=dst, send_sem=s, recv_sem=d, device_id=to, device_id_type=MESH
        ).start()

    drains = []

    def finish():
        for condition, ref, sem in drains:
            if condition is None:
                wait_for(ref, sem)
            else:

                @pl.when(condition)
                def _():
                    wait_for(ref, sem)

    def in_line(f):
        return lax.rem(f, nx) * nz + f // nx

    order = [2 * chip(s) + 1 - c for s in shifts] + [2 * chip(s) + c for s in shifts]
    loads = []

    def load(k):
        two = pl.ds(pl.multiple_of(chip(shifts[k]) * 2 * width, LANES), 2 * width)
        copies = [
            pltpu.make_async_copy(src.at[:, :, two], dst.at[:, :, two], load_sem.at[k, i])
            for i, (src, dst) in enumerate(((lp_hbm, cor), (base_hbm, basev), (err_hbm, errv)))
        ]
        for copy in copies:
            copy.start()
        loads.append(copies)

    load(0)
    barrier = pltpu.get_barrier_semaphore()

    def greet(replica, there):
        pl.semaphore_signal(barrier, inc=1, device_id={"replica": replica, "fsdp": there}, device_id_type=MESH)

    for k in range(1, replicas):
        greet(lax.rem(r + k, replicas), f)
    for k in range(1, nx):
        greet(2 * y + 1 - c, z * nx + lax.rem(x + k, nx))
    for k in range(1, fsdp):
        greet(r, lax.rem(f + k, fsdp))
    for k in range(1, chips):
        load(k)
    load_momentum = pltpu.make_async_copy(mom_hbm, momv, mom_sem.at[0])

    def correct(n):
        if n < chips:
            for copy in loads[n]:
                copy.wait()
        at_cols = cols(order[n])
        cor[:, :, at_cols] = basev[:, :, at_cols] - cor[:, :, at_cols] + errv[:, :, at_cols]

    for k in range(chips):
        write_start_factor(seed_ref[0], order[chips + k] * width, start.at[k])
        correct(k)
        if k == 0:
            pl.semaphore_wait(barrier, replicas - 1 + nx - 1 + fsdp - 1)
        send(cor.at[:, :, cols(order[k])], sib.at[k], p1_send.at[k], p1_recv.at[k], sibling)
    load_momentum.start()
    for k in range(chips):
        correct(chips + k)

    def paired(k):
        wait_for(sib.at[k], p1_recv.at[k])
        sib[k] = sib[k] + cor[:, :, cols(order[chips + k])]

    def hop(n, src, dst, shift):
        send(src, dst, p2_send.at[n], p2_recv.at[n], along_y(shift))
        drains.append((None, src, p2_send.at[n]))

    paired(0)
    hop(0, sib.at[0, 0], relay.at[0], 1)
    hop(1, sib.at[0, 1], relay.at[1], 3)

    scale = 3.4641016 / 65521.0 / 2.0 / replicas
    left_terms = times_start_factor(sib[0].reshape(rows, width), start[0])
    for k in range(1, chips):
        paired(k)
        left_terms = left_terms + times_start_factor(sib[k].reshape(rows, width), start[k])
    part[...] = (left_terms * scale).reshape(part.shape)
    parts[r] = part[c]
    for k in range(1, replicas):
        to = lax.rem(r + k, replicas)
        send(part.at[lax.rem(to, 2)], parts.at[r], p3_sem.at[0], p3_sem.at[1], {"replica": to, "fsdp": f})
    drains.append((None, parts.at[pl.ds(0, replicas - 1)], p3_sem.at[0]))

    hop(2, sib.at[1, 1], rs.at[0, 1], 1)
    hop(3, sib.at[2, 0], rs.at[1, 0], 3)
    wait_for(relay.at[0], p2_recv.at[0])
    relay[0] = relay[0] + sib[1, 0]
    hop(4, relay.at[0], rs.at[0, 0], 1)
    wait_for(relay.at[1], p2_recv.at[1])
    relay[1] = relay[1] + sib[2, 1]
    hop(5, relay.at[1], rs.at[1, 1], 3)

    wait_for(parts.at[pl.ds(0, replicas - 1)], p3_sem.at[1])
    total = parts[0]
    for k in range(1, replicas):
        total = total + parts[k]
    line[z] = total

    has_tile, my_tile = tile_of(f, 2 * tiles, fsdp)
    owner = jnp.logical_and(has_tile, lax.rem(my_tile, 2) == c)
    other = jnp.logical_not(owner)
    my_tile = my_tile // 2

    def to_owner(t):
        to = owner_of(2 * t + c, 2 * tiles, fsdp)
        tile = blk.at[t]

        @pl.when(to != f)
        def _():
            send(tile, at.at[in_line(f)], p5_sem.at[0], p5_sem.at[1], {"replica": r, "fsdp": to})

        @pl.when(to == f)
        def _():
            at[in_line(f)] = tile[...]

    for k in range(1, nz):
        to = lax.rem(z + k, nz) * nx + x
        send(line.at[z], line.at[z], pz_sem.at[0], pz_sem.at[1], {"replica": r, "fsdp": to})
    drains.append((None, line.at[pl.ds(0, nz - 1)], pz_sem.at[0]))
    wait_for(line.at[pl.ds(0, nz - 1)], pz_sem.at[1])
    for k in range(nx):
        there = z * nx + lax.rem(x + k, nx)
        has, tile = tile_of(there, 2 * tiles, fsdp)
        core = lax.rem(tile, 2)
        remote = has if k else jnp.logical_and(has, core != c)

        @pl.when(remote)
        def _():
            send(line, left.at[c * nx + x], px_send.at[k], px_recv.at[0], {"replica": 2 * y + core, "fsdp": there})

        drains.append((remote, line, px_send.at[k]))
    for n, (a, b) in zip((2, 3, 4, 5), ((0, 1), (1, 0), (0, 0), (1, 1)), strict=True):
        wait_for(rs.at[a, b], p2_recv.at[n])
    mean = (sib[3] + rs[0] + rs[1]) * (1.0 / replicas)
    for t in range(tiles):
        blk[t] = mean[:, :, t * LANES : (t + 1) * LANES]
    for t in range(tiles):
        to_owner(t)
    drains.append((owner, at.at[pl.ds(0, tiles - 1)], p5_sem.at[0]))
    drains.append((other, at.at[pl.ds(0, tiles)], p5_sem.at[0]))

    cut = tiles // 2
    sizes = (cut, tiles - cut)
    my_half = my_tile // cut
    my_tile = r * tiles + my_tile

    @pl.when(owner)
    def _():
        left[c * nx + x] = line[...]
        wait_for(left.at[pl.ds(0, 2 * nx - 1)], px_recv.at[0])
        whole = left[...].reshape(fsdp * rows, RANK)
        against = (((0,), (0,)), ((), ()))
        mg[...] = lax.dot_general(
            whole, whole, against, precision=HIGHEST, preferred_element_type=jnp.float32
        ).reshape(mg.shape)
        invert(mg)
        wait_for(at.at[pl.ds(0, fsdp - 1)], p5_sem.at[1])

        def left_half(h):
            return left[pl.ds(h * nx, nx)].reshape(fsdp * half, RANK)

        products = [
            lax.dot_general(
                left_half(h),
                at[:, h].reshape(fsdp * half, LANES),
                against,
                precision=HIGHEST,
                preferred_element_type=jnp.float32,
            )
            for h in range(2)
        ]
        weights = jnp.dot(
            mg[...].reshape(RANK, RANK),
            products[0] + products[1],
            precision=HIGHEST,
            preferred_element_type=jnp.float32,
        )
        for h in range(2):
            ap[:, h] = jnp.dot(
                left_half(h), weights, precision=HIGHEST, preferred_element_type=jnp.float32
            ).reshape(fsdp, half, LANES)

        def give(k, _):
            to = lax.rem(f + k, fsdp)
            send(ap.at[in_line(to)], apx.at[my_tile], p7_send.at[0], p7_recv.at[my_half], {"replica": r, "fsdp": to})
            return 0

        lax.fori_loop(1, fsdp, give, 0)
        apx[my_tile] = ap[in_line(f)]

    def returned(h):
        mine_too = jnp.logical_and(owner, my_half == h)

        @pl.when(mine_too)
        def _():
            wait_for(apx.at[pl.ds(0, sizes[h] - 1)], p7_recv.at[h])

        @pl.when(jnp.logical_not(mine_too))
        def _():
            wait_for(apx.at[pl.ds(0, sizes[h])], p7_recv.at[h])

    drains.append((owner, ap.at[pl.ds(0, fsdp - 1)], p7_send.at[0]))
    def place(block, h):
        return apx.at[pl.ds(block * tiles + h * cut, sizes[h])]

    def end(block, h):
        for t in range(sizes[h]):
            tile = block * tiles + h * cut + t
            at_cols = pl.ds(pl.multiple_of(tile * LANES, LANES), LANES)
            found = apx[tile]
            cor[:, :, at_cols] = cor[:, :, at_cols] - found
            momentum = 0.9 * momv[:, :, at_cols] + found
            momv[:, :, at_cols] = momentum
            basev[:, :, at_cols] = basev[:, :, at_cols] - 0.7 * (found + 0.9 * momentum)

    def pass_on(h):
        for k, shift in enumerate(shifts[:-1]):
            send(place(r, h), place(r, h), p8_send.at[h, k], p8_recv.at[h, k], along_y(shift))
            drains.append((None, place(r, h), p8_send.at[h, k]))
        send(place(r, h), place(r, h), p9_send.at[h, chips - 1], p9_recv.at[h, chips - 1], sibling)
        drains.append((None, place(r, h), p9_send.at[h, chips - 1]))

    returned(0)
    pass_on(0)
    load_momentum.wait()
    for k in range(chips):
        wait_for(sib.at[k], p1_send.at[k])
    end(r, 0)
    returned(1)
    pass_on(1)
    end(r, 1)
    for h in range(2):
        for k in (1, 2, 0):
            block = 2 * chip(chips - shifts[k]) + c
            wait_for(place(block, h), p8_recv.at[h, k])
            send(place(block, h), place(block, h), p9_send.at[h, k], p9_recv.at[h, k], sibling)
            drains.append((None, place(block, h), p9_send.at[h, k]))
            end(block, h)
        for k in (3, 1, 2, 0):
            block = 2 * chip(chips - shifts[k]) + 1 - c
            wait_for(place(block, h), p9_recv.at[h, k])
            end(block, h)
    finish()


def on_device(local_params, outer_base, error_memory, momentum, start_seed):
    replicas, fsdp = lax.axis_size("replica"), lax.axis_size("fsdp")
    rows, columns = outer_base.shape
    half = rows // 2
    tiles = columns // replicas // LANES
    width = tiles * LANES
    chips = replicas // 2
    f32 = jnp.float32
    whole = (2, half, columns)
    dma = pltpu.SemaphoreType.DMA
    in_hbm = pl.BlockSpec(memory_space=pltpu.HBM)
    new_error, new_base, new_momentum = pl.pallas_call(
        functools.partial(kernel, replicas, fsdp, tiles),
        out_shape=[pltpu.VMEM(whole, f32)] * 3,
        in_specs=[pl.BlockSpec(memory_space=pltpu.SMEM), in_hbm, in_hbm, in_hbm, in_hbm],
        out_specs=[pl.BlockSpec(memory_space=pltpu.VMEM)] * 3,
        scratch_shapes=[
            pltpu.VMEM(whole, f32),
            pltpu.VMEM((chips, 2, half, width), f32),
            pltpu.VMEM((2, half, width), f32),
            pltpu.VMEM((2, 2, half, width), f32),
            pltpu.VMEM((tiles, 2, half, LANES), f32),
            pltpu.VMEM((chips, width, 2 * RANK), jnp.bfloat16),
            pltpu.VMEM((2, half, RANK), f32),
            pltpu.VMEM((replicas, half, RANK), f32),
            pltpu.VMEM((fsdp // along_x(fsdp), half, RANK), f32),
            pltpu.VMEM((2 * along_x(fsdp), fsdp // along_x(fsdp), half, RANK), f32),
            pltpu.VMEM((fsdp, 2, half, LANES), f32),
            pltpu.VMEM((fsdp, 2, half, LANES), f32),
            pltpu.VMEM((columns // LANES, 2, half, LANES), f32),
            pltpu.VMEM((RANK // SUBS, SUBS, RANK), f32),
            dma((chips, 3)),
            dma((1,)),
            dma((chips,)),
            dma((chips,)),
            dma((6,)),
            dma((6,)),
            dma((2,)),
            dma((2,)),
            dma((4,)),
            dma((1,)),
            dma((2,)),
            dma((1,)),
            dma((2,)),
            dma((2, chips)),
            dma((2, chips)),
            dma((2, chips)),
            dma((2, chips)),
        ],
        compiler_params=pltpu.CompilerParams(
            collective_id=0, has_side_effects=True, vmem_limit_bytes=60 * 1024 * 1024
        ),
        cost_estimate=pl.CostEstimate(flops=10**9, bytes_accessed=4 * 10**6, transcendentals=0),
        name="approximate",
    )(
        start_seed,
        local_params.reshape(whole),
        outer_base.reshape(whole),
        error_memory.reshape(whole),
        momentum.reshape(whole),
    )
    return (new_error.reshape(1, rows, columns), new_base.reshape(rows, columns), new_momentum.reshape(rows, columns))


def solution(mesh):
    placed = (
        P("replica", "fsdp", None),
        P("fsdp", None),
        P("replica", "fsdp", None),
        P("fsdp", None),
        P(),
    )
    return jax.shard_map(
        on_device,
        mesh=mesh,
        in_specs=placed,
        out_specs=(P("replica", "fsdp", None), P("fsdp", None), P("fsdp", None)),
        check_vma=False,
    )
```

```python
import functools

import jax
import jax.numpy as jnp
from jax import lax
from jax.experimental import pallas as pl
from jax.experimental.pallas import tpu as pltpu
from jax.sharding import PartitionSpec as P

RANK = 128
LANES = 128
SUBS = 8
HIGHEST = lax.Precision.HIGHEST
MESH = pl.DeviceIdType.MESH


def owner_of(tile, tiles, fsdp):
    return tile if tiles == fsdp else tile + 1 + tile // 8


def tile_of(f, tiles, fsdp):
    if tiles == fsdp:
        return f >= 0, f
    tile = f - 1 - f // 9
    return jnp.logical_and(lax.rem(f, 9) != 0, tile < tiles), tile


def write_start_factor(seed, first_row, out_ref):
    two = 2 * SUBS
    k = lax.broadcasted_iota(jnp.int32, (two, LANES), 1)
    j = lax.broadcasted_iota(jnp.int32, (two, LANES), 0) + first_row
    mixed = lax.rem(181 * j + 359 * k + 1013 * seed, 65521)
    added = 7 * j + 3 * k

    def rows(i, carry):
        mixed, added = carry
        low = jnp.where(mixed >= 65498, mixed - 65498, jnp.where(mixed >= 32749, mixed - 32749, mixed))
        value = mixed * low + added
        quotient = (value.astype(jnp.float32) * ((1.0 - 2.0**-21) / 65521.0)).astype(jnp.int32)
        rest = value - quotient * 65521
        rest = jnp.where(rest >= 65521, rest - 65521, rest)
        odd = 2 * rest - 65521
        high = (odd + 256) >> 9
        here = pl.ds(pl.multiple_of(i * two, two), two)
        out_ref[here, :LANES] = high.astype(jnp.float32).astype(jnp.bfloat16)
        out_ref[here, LANES:] = (odd - 512 * high).astype(jnp.float32).astype(jnp.bfloat16)
        mixed = mixed + 181 * two
        return jnp.where(mixed >= 65521, mixed - 65521, mixed), added + 7 * two

    lax.fori_loop(0, out_ref.shape[0] // two, rows, (mixed, added), unroll=8)


def times_start_factor(x, start):
    parts, rest = [], x
    for _ in range(3):
        parts.append(rest.astype(jnp.bfloat16))
        rest = rest - parts[-1].astype(jnp.float32)
    both = jnp.dot(jnp.concatenate(parts, axis=0), start, preferred_element_type=jnp.float32)
    wide = 512.0 * both[:, :LANES] + both[:, LANES:]
    n = x.shape[0]
    return (wide[2 * n :] + wide[n : 2 * n]) + wide[:n]


def invert(m):
    sub = lax.broadcasted_iota(jnp.int32, (SUBS, LANES), 0)
    lane = lax.broadcasted_iota(jnp.int32, (SUBS, LANES), 1)

    def col(x, at):
        return jnp.broadcast_to(x[:, at : at + 1], (SUBS, LANES))

    def row(x, i):
        return jnp.broadcast_to(x[i : i + 1, :], (SUBS, LANES))

    panels = RANK // SUBS
    for p in range(panels):
        first = SUBS * p
        x = m[p]
        cols = [col(x, first + j) for j in range(SUBS)]
        inside = jnp.logical_and(lane >= first, lane < first + SUBS)
        x = jnp.where(inside, jnp.where(lane - first == sub, 1.0, 0.0), x)
        for i in range(SUBS):
            scale = 1.0 / row(cols[i], i)
            here = sub == i
            by = cols[i]

            def step(x):
                pivot_row = row(x, i) * scale
                return jnp.where(here, pivot_row, x - by * pivot_row)

            x = step(x)
            for j in range(i + 1, SUBS):
                cols[j] = step(cols[j])
        rows = [row(x, j) for j in range(SUBS)]
        for q in [(p + 1 + k) % panels for k in range(panels - 1)]:
            a = m[q]
            t = [col(a, first + j) * rows[j] for j in range(SUBS)]
            taken = ((t[0] + t[1]) + (t[2] + t[3])) + ((t[4] + t[5]) + (t[6] + t[7]))
            m[q] = jnp.where(inside, 0.0, a) - taken
        m[p] = x


def along_x(fsdp):
    return 4 if fsdp % 8 == 0 else 2


def wait_for(ref, sem):
    if 0 in ref.shape:
        return
    pltpu.make_async_copy(ref, ref, sem).wait()


def kernel(
    replicas, fsdp, tiles,
    seed_ref, lp_hbm, base_hbm, err_hbm, mom_hbm, cor, basev, momv, out,
    errv, sib, relay, rs, blk, start, part, parts, line, left, at, ap, apx, mg,
    load_sem, mom_sem, p1_send, p1_recv, p2_send, p2_recv, p3_sem, pz_sem, px_send, px_recv, p5_sem, p7_send, p7_recv,
    p8_send, p8_recv, p9_send, p9_recv,
):
    chips = replicas // 2
    width = tiles * LANES
    half = blk.shape[2]
    rows = 2 * half
    r = lax.axis_index("replica")
    f = lax.axis_index("fsdp")
    c = lax.rem(r, 2)
    y = r // 2
    nx = along_x(fsdp)
    nz = fsdp // nx
    z, x = f // nx, lax.rem(f, nx)
    far_first = [
        (dz, dx)
        for dz in sorted(range(nz), key=lambda k: -min(k, nz - k))
        for dx in range(nx)
        if dz or dx
    ]
    sibling = {"replica": 2 * y + 1 - c, "fsdp": f}
    shifts = [2, 1, 3, 0]

    def cols(block):
        return pl.ds(pl.multiple_of(block * width, LANES), width)

    def chip(shift):
        return lax.rem(y + shift, chips)

    def along_y(shift):
        return {"replica": 2 * chip(shift) + c, "fsdp": f}

    def send(src, dst, s, d, to):
        pltpu.make_async_remote_copy(
            src_ref=src, dst_ref=dst, send_sem=s, recv_sem=d, device_id=to, device_id_type=MESH
        ).start()

    drains = []

    def finish():
        for condition, ref, sem in drains:
            if condition is None:
                wait_for(ref, sem)
            else:

                @pl.when(condition)
                def _():
                    wait_for(ref, sem)

    def in_line(f):
        return lax.rem(f, nx) * nz + f // nx

    order = [2 * chip(s) + 1 - c for s in shifts] + [2 * chip(s) + c for s in shifts]
    loads = []

    def load(k):
        two = pl.ds(pl.multiple_of(chip(shifts[k]) * 2 * width, LANES), 2 * width)
        copies = [
            pltpu.make_async_copy(src.at[:, :, two], dst.at[:, :, two], load_sem.at[k, i])
            for i, (src, dst) in enumerate(((lp_hbm, cor), (base_hbm, basev), (err_hbm, errv)))
        ]
        for copy in copies:
            copy.start()
        loads.append(copies)

    load(0)
    barrier = pltpu.get_barrier_semaphore()

    def greet(replica, there):
        pl.semaphore_signal(barrier, inc=1, device_id={"replica": replica, "fsdp": there}, device_id_type=MESH)

    for k in range(1, replicas):
        greet(lax.rem(r + k, replicas), f)
    for k in range(1, nx):
        greet(2 * y + 1 - c, z * nx + lax.rem(x + k, nx))
    for k in range(1, fsdp):
        greet(r, lax.rem(f + k, fsdp))
    for k in range(1, chips):
        load(k)
    load_momentum = pltpu.make_async_copy(mom_hbm, momv, mom_sem.at[0])

    def correct(n):
        if n < chips:
            for copy in loads[n]:
                copy.wait()
        at_cols = cols(order[n])
        cor[:, :, at_cols] = basev[:, :, at_cols] - cor[:, :, at_cols] + errv[:, :, at_cols]

    for k in range(chips):
        write_start_factor(seed_ref[0], order[chips + k] * width, start.at[k])
        correct(k)
        if k == 0:
            pl.semaphore_wait(barrier, replicas - 1 + nx - 1 + fsdp - 1)
        send(cor.at[:, :, cols(order[k])], sib.at[k], p1_send.at[k], p1_recv.at[k], sibling)
    load_momentum.start()
    for k in range(chips):
        correct(chips + k)

    def paired(k):
        wait_for(sib.at[k], p1_recv.at[k])
        sib[k] = sib[k] + cor[:, :, cols(order[chips + k])]

    def hop(n, src, dst, shift):
        send(src, dst, p2_send.at[n], p2_recv.at[n], along_y(shift))
        drains.append((None, src, p2_send.at[n]))

    paired(0)
    hop(0, sib.at[0, 0], relay.at[0], 1)
    hop(1, sib.at[0, 1], relay.at[1], 3)

    scale = 3.4641016 / 65521.0 / 2.0 / replicas
    left_terms = times_start_factor(sib[0].reshape(rows, width), start[0])
    for k in range(1, chips):
        paired(k)
        if k == 1:
            hop(2, sib.at[1, 1], rs.at[0, 1], 1)
        if k == 2:
            hop(3, sib.at[2, 0], rs.at[1, 0], 3)
        left_terms = left_terms + times_start_factor(sib[k].reshape(rows, width), start[k])
    part[...] = (left_terms * scale).reshape(part.shape)
    parts[r] = part[c]
    for k in sorted(range(1, replicas), key=lambda k: -min(k, replicas - k)):
        to = lax.rem(r + k, replicas)
        send(part.at[lax.rem(to, 2)], parts.at[r], p3_sem.at[0], p3_sem.at[1], {"replica": to, "fsdp": f})
    drains.append((None, parts.at[pl.ds(0, replicas - 1)], p3_sem.at[0]))

    wait_for(relay.at[0], p2_recv.at[0])
    relay[0] = relay[0] + sib[1, 0]
    hop(4, relay.at[0], rs.at[0, 0], 1)
    wait_for(relay.at[1], p2_recv.at[1])
    relay[1] = relay[1] + sib[2, 1]
    hop(5, relay.at[1], rs.at[1, 1], 3)

    wait_for(parts.at[pl.ds(0, replicas - 1)], p3_sem.at[1])
    total = parts[0]
    for k in range(1, replicas):
        total = total + parts[k]
    line[z] = total

    has_tile, my_tile = tile_of(f, 2 * tiles, fsdp)
    owner = jnp.logical_and(has_tile, lax.rem(my_tile, 2) == c)
    other = jnp.logical_not(owner)
    my_tile = my_tile // 2

    def to_owner(t):
        to = owner_of(2 * t + c, 2 * tiles, fsdp)
        tile = blk.at[t]

        @pl.when(to != f)
        def _():
            send(tile, at.at[in_line(f)], p5_sem.at[0], p5_sem.at[1], {"replica": r, "fsdp": to})

        @pl.when(to == f)
        def _():
            at[in_line(f)] = tile[...]

    for k in sorted(range(1, nz), key=lambda k: -min(k, nz - k)):
        to = lax.rem(z + k, nz) * nx + x
        send(line.at[z], line.at[z], pz_sem.at[0], pz_sem.at[1], {"replica": r, "fsdp": to})
    drains.append((None, line.at[pl.ds(0, nz - 1)], pz_sem.at[0]))
    for n, (a, b) in zip((2, 3, 4, 5), ((0, 1), (1, 0), (0, 0), (1, 1)), strict=True):
        wait_for(rs.at[a, b], p2_recv.at[n])
    mean = (sib[3] + rs[0] + rs[1]) * (1.0 / replicas)
    for t in range(tiles):
        blk[t] = mean[:, :, t * LANES : (t + 1) * LANES]
    for t in range(tiles):
        to_owner(lax.rem(t + f * tiles // fsdp, tiles))
    wait_for(line.at[pl.ds(0, nz - 1)], pz_sem.at[1])
    for k in sorted(range(nx), key=lambda k: -min(k, nx - k)):
        there = z * nx + lax.rem(x + k, nx)
        has, tile = tile_of(there, 2 * tiles, fsdp)
        core = lax.rem(tile, 2)
        remote = has if k else jnp.logical_and(has, core != c)

        @pl.when(remote)
        def _():
            send(line, left.at[c * nx + x], px_send.at[k], px_recv.at[0], {"replica": 2 * y + core, "fsdp": there})

        drains.append((remote, line, px_send.at[k]))
    drains.append((owner, at.at[pl.ds(0, tiles - 1)], p5_sem.at[0]))
    drains.append((other, at.at[pl.ds(0, tiles)], p5_sem.at[0]))

    cut = tiles // 2
    sizes = (cut, tiles - cut)
    my_half = my_tile // cut
    my_tile = r * tiles + my_tile

    @pl.when(owner)
    def _():
        left[c * nx + x] = line[...]
        wait_for(left.at[pl.ds(0, 2 * nx - 1)], px_recv.at[0])
        whole = left[...].reshape(fsdp * rows, RANK)
        against = (((0,), (0,)), ((), ()))
        mg[...] = lax.dot_general(
            whole, whole, against, precision=HIGHEST, preferred_element_type=jnp.float32
        ).reshape(mg.shape)
        invert(mg)
        wait_for(at.at[pl.ds(0, fsdp - 1)], p5_sem.at[1])

        def left_half(h):
            return left[pl.ds(h * nx, nx)].reshape(fsdp * half, RANK)

        products = [
            lax.dot_general(
                left_half(h),
                at[:, h].reshape(fsdp * half, LANES),
                against,
                precision=HIGHEST,
                preferred_element_type=jnp.float32,
            )
            for h in range(2)
        ]
        weights = jnp.dot(
            mg[...].reshape(RANK, RANK),
            products[0] + products[1],
            precision=HIGHEST,
            preferred_element_type=jnp.float32,
        )
        for h in range(2):
            ap[:, h] = jnp.dot(
                left_half(h), weights, precision=HIGHEST, preferred_element_type=jnp.float32
            ).reshape(fsdp, half, LANES)

        def give(dz, dx):
            to = lax.rem(z + dz, nz) * nx + lax.rem(x + dx, nx)
            send(ap.at[in_line(to)], apx.at[my_tile], p7_send.at[0], p7_recv.at[my_half], {"replica": r, "fsdp": to})
            return 0

        for dz, dx in far_first:
            give(dz, dx)
        apx[my_tile] = ap[in_line(f)]

    def returned(h):
        mine_too = jnp.logical_and(owner, my_half == h)

        @pl.when(mine_too)
        def _():
            wait_for(apx.at[pl.ds(0, sizes[h] - 1)], p7_recv.at[h])

        @pl.when(jnp.logical_not(mine_too))
        def _():
            wait_for(apx.at[pl.ds(0, sizes[h])], p7_recv.at[h])

    drains.append((owner, ap.at[pl.ds(0, fsdp - 1)], p7_send.at[0]))
    def place(block, h):
        return apx.at[pl.ds(block * tiles + h * cut, sizes[h])]

    def end(block, h):
        for t in range(sizes[h]):
            tile = block * tiles + h * cut + t
            at_cols = pl.ds(pl.multiple_of(tile * LANES, LANES), LANES)
            out[:, :, at_cols] = apx[tile]

    def pass_on(h):
        for k, shift in enumerate(shifts[:-1]):
            send(place(r, h), place(r, h), p8_send.at[h, k], p8_recv.at[h, k], along_y(shift))
            drains.append((None, place(r, h), p8_send.at[h, k]))
        send(place(r, h), place(r, h), p9_send.at[h, chips - 1], p9_recv.at[h, chips - 1], sibling)
        drains.append((None, place(r, h), p9_send.at[h, chips - 1]))

    returned(0)
    pass_on(0)
    load_momentum.wait()
    for k in range(chips):
        wait_for(sib.at[k], p1_send.at[k])
    end(r, 0)
    returned(1)
    pass_on(1)
    end(r, 1)
    for h in range(2):
        for k in (1, 2, 0):
            block = 2 * chip(chips - shifts[k]) + c
            wait_for(place(block, h), p8_recv.at[h, k])
            send(place(block, h), place(block, h), p9_send.at[h, k], p9_recv.at[h, k], sibling)
            drains.append((None, place(block, h), p9_send.at[h, k]))
            end(block, h)
        for k in (3, 1, 2, 0):
            block = 2 * chip(chips - shifts[k]) + 1 - c
            wait_for(place(block, h), p9_recv.at[h, k])
            end(block, h)
    finish()


def on_device(local_params, outer_base, error_memory, momentum, start_seed):
    replicas, fsdp = lax.axis_size("replica"), lax.axis_size("fsdp")
    rows, columns = outer_base.shape
    half = rows // 2
    tiles = columns // replicas // LANES
    width = tiles * LANES
    chips = replicas // 2
    f32 = jnp.float32
    whole = (2, half, columns)
    dma = pltpu.SemaphoreType.DMA
    in_hbm = pl.BlockSpec(memory_space=pltpu.HBM)
    corrected, base, old_momentum, approx = pl.pallas_call(
        functools.partial(kernel, replicas, fsdp, tiles),
        out_shape=[pltpu.VMEM(whole, f32)] * 4,
        in_specs=[pl.BlockSpec(memory_space=pltpu.SMEM), in_hbm, in_hbm, in_hbm, in_hbm],
        out_specs=[pl.BlockSpec(memory_space=pltpu.VMEM)] * 4,
        scratch_shapes=[
            pltpu.VMEM(whole, f32),
            pltpu.VMEM((chips, 2, half, width), f32),
            pltpu.VMEM((2, half, width), f32),
            pltpu.VMEM((2, 2, half, width), f32),
            pltpu.VMEM((tiles, 2, half, LANES), f32),
            pltpu.VMEM((chips, width, 2 * RANK), jnp.bfloat16),
            pltpu.VMEM((2, half, RANK), f32),
            pltpu.VMEM((replicas, half, RANK), f32),
            pltpu.VMEM((fsdp // along_x(fsdp), half, RANK), f32),
            pltpu.VMEM((2 * along_x(fsdp), fsdp // along_x(fsdp), half, RANK), f32),
            pltpu.VMEM((fsdp, 2, half, LANES), f32),
            pltpu.VMEM((fsdp, 2, half, LANES), f32),
            pltpu.VMEM((columns // LANES, 2, half, LANES), f32),
            pltpu.VMEM((RANK // SUBS, SUBS, RANK), f32),
            dma((chips, 3)),
            dma((1,)),
            dma((chips,)),
            dma((chips,)),
            dma((6,)),
            dma((6,)),
            dma((2,)),
            dma((2,)),
            dma((4,)),
            dma((1,)),
            dma((2,)),
            dma((1,)),
            dma((2,)),
            dma((2, chips)),
            dma((2, chips)),
            dma((2, chips)),
            dma((2, chips)),
        ],
        compiler_params=pltpu.CompilerParams(
            collective_id=0, has_side_effects=True, vmem_limit_bytes=59 * 1024 * 1024
        ),
        cost_estimate=pl.CostEstimate(flops=10**9, bytes_accessed=4 * 10**6, transcendentals=0),
        name="approximate",
    )(
        start_seed,
        local_params.reshape(whole),
        outer_base.reshape(whole),
        error_memory.reshape(whole),
        momentum.reshape(whole),
    )
    new_error = corrected - approx
    new_momentum = 0.9 * old_momentum + approx
    new_base = base - 0.7 * (approx + 0.9 * new_momentum)
    return (new_error.reshape(1, rows, columns), new_base.reshape(rows, columns), new_momentum.reshape(rows, columns))


def solution(mesh):
    placed = (
        P("replica", "fsdp", None),
        P("fsdp", None),
        P("replica", "fsdp", None),
        P("fsdp", None),
        P(),
    )
    return jax.shard_map(
        on_device,
        mesh=mesh,
        in_specs=placed,
        out_specs=(P("replica", "fsdp", None), P("fsdp", None), P("fsdp", None)),
        check_vma=False,
    )
```

```python
import functools

import jax
import jax.numpy as jnp
from jax import lax
from jax.experimental import pallas as pl
from jax.experimental.pallas import tpu as pltpu
from jax.sharding import PartitionSpec as P

RANK = 128
LANES = 128
SUBS = 8
HIGHEST = lax.Precision.HIGHEST
MESH = pl.DeviceIdType.MESH


def owner_of(tile, tiles, fsdp):
    return tile if tiles == fsdp else tile + 1 + tile // 8


def tile_of(f, tiles, fsdp):
    if tiles == fsdp:
        return f >= 0, f
    tile = f - 1 - f // 9
    return jnp.logical_and(lax.rem(f, 9) != 0, tile < tiles), tile


def write_start_factor(seed, first_row, out_ref):
    two = 2 * SUBS
    k = lax.broadcasted_iota(jnp.int32, (two, LANES), 1)
    j = lax.broadcasted_iota(jnp.int32, (two, LANES), 0) + first_row
    mixed = lax.rem(181 * j + 359 * k + 1013 * seed, 65521)
    added = 7 * j + 3 * k

    def rows(i, carry):
        mixed, added = carry
        low = jnp.where(mixed >= 65498, mixed - 65498, jnp.where(mixed >= 32749, mixed - 32749, mixed))
        value = mixed * low + added
        quotient = (value.astype(jnp.float32) * ((1.0 - 2.0**-21) / 65521.0)).astype(jnp.int32)
        rest = value - quotient * 65521
        rest = jnp.where(rest >= 65521, rest - 65521, rest)
        odd = 2 * rest - 65521
        high = (odd + 256) >> 9
        here = pl.ds(pl.multiple_of(i * two, two), two)
        out_ref[here, :LANES] = high.astype(jnp.float32).astype(jnp.bfloat16)
        out_ref[here, LANES:] = (odd - 512 * high).astype(jnp.float32).astype(jnp.bfloat16)
        mixed = mixed + 181 * two
        return jnp.where(mixed >= 65521, mixed - 65521, mixed), added + 7 * two

    lax.fori_loop(0, out_ref.shape[0] // two, rows, (mixed, added), unroll=8)


def times_start_factor(x, start):
    parts, rest = [], x
    for _ in range(3):
        parts.append(rest.astype(jnp.bfloat16))
        rest = rest - parts[-1].astype(jnp.float32)
    both = jnp.dot(jnp.concatenate(parts, axis=0), start, preferred_element_type=jnp.float32)
    wide = 512.0 * both[:, :LANES] + both[:, LANES:]
    n = x.shape[0]
    return (wide[2 * n :] + wide[n : 2 * n]) + wide[:n]


def invert(m):
    sub = lax.broadcasted_iota(jnp.int32, (SUBS, LANES), 0)
    lane = lax.broadcasted_iota(jnp.int32, (SUBS, LANES), 1)

    def col(x, at):
        return jnp.broadcast_to(x[:, at : at + 1], (SUBS, LANES))

    def row(x, i):
        return jnp.broadcast_to(x[i : i + 1, :], (SUBS, LANES))

    panels = RANK // SUBS
    for p in range(panels):
        first = SUBS * p
        x = m[p]
        cols = [col(x, first + j) for j in range(SUBS)]
        inside = jnp.logical_and(lane >= first, lane < first + SUBS)
        x = jnp.where(inside, jnp.where(lane - first == sub, 1.0, 0.0), x)
        scales = jnp.ones_like(x)
        for i in range(SUBS):
            pivot = row(cols[i], i)
            scale = 1.0 / pivot
            scales = jnp.where(sub == i, scale, scales)
            by = jnp.where(sub == i, 0.0, cols[i])

            def step(x):
                return x - by * (row(x, i) * scale)

            x = step(x)
            for j in range(i + 1, SUBS):
                cols[j] = step(cols[j])
        x = x * scales
        rows = [row(x, j) for j in range(SUBS)]
        for q in [(p + 1 + k) % panels for k in range(panels - 1)]:
            a = m[q]
            t = [col(a, first + j) * rows[j] for j in range(SUBS)]
            taken = ((t[0] + t[1]) + (t[2] + t[3])) + ((t[4] + t[5]) + (t[6] + t[7]))
            m[q] = jnp.where(inside, 0.0, a) - taken
        m[p] = x


def along_x(fsdp):
    return 4 if fsdp % 8 == 0 else 2


def wait_for(ref, sem):
    if 0 in ref.shape:
        return
    pltpu.make_async_copy(ref, ref, sem).wait()


def kernel(
    replicas, fsdp, tiles,
    seed_ref, lp_hbm, base_hbm, err_hbm, mom_hbm, cor, basev, momv, out,
    errv, sib, relay, rs, blk, start, part, parts, line, left, at, ap, apx, mg,
    load_sem, mom_sem, p1_send, p1_recv, p2_send, p2_recv, p3_sem, pz_sem, px_send, px_recv, p5_sem, p7_send, p7_recv,
    p8_send, p8_recv, p9_send, p9_recv,
):
    chips = replicas // 2
    width = tiles * LANES
    half = blk.shape[2]
    rows = 2 * half
    r = lax.axis_index("replica")
    f = lax.axis_index("fsdp")
    c = lax.rem(r, 2)
    y = r // 2
    nx = along_x(fsdp)
    nz = fsdp // nx
    z, x = f // nx, lax.rem(f, nx)
    far_first = [
        (dz, dx)
        for dz in sorted(range(nz), key=lambda k: -min(k, nz - k))
        for dx in sorted(range(nx), key=lambda k: -min(k, nx - k))
        if dz or dx
    ]
    sibling = {"replica": 2 * y + 1 - c, "fsdp": f}
    shifts = [2, 1, 3, 0]

    def cols(block):
        return pl.ds(pl.multiple_of(block * width, LANES), width)

    def chip(shift):
        return lax.rem(y + shift, chips)

    def along_y(shift):
        return {"replica": 2 * chip(shift) + c, "fsdp": f}

    def send(src, dst, s, d, to):
        pltpu.make_async_remote_copy(
            src_ref=src, dst_ref=dst, send_sem=s, recv_sem=d, device_id=to, device_id_type=MESH
        ).start()

    drains = []

    def finish():
        for condition, ref, sem in drains:
            if condition is None:
                wait_for(ref, sem)
            else:

                @pl.when(condition)
                def _():
                    wait_for(ref, sem)

    def in_line(f):
        return lax.rem(f, nx) * nz + f // nx

    order = [2 * chip(s) + 1 - c for s in shifts] + [2 * chip(s) + c for s in shifts]
    loads = []

    def load(k):
        two = pl.ds(pl.multiple_of(chip(shifts[k]) * 2 * width, LANES), 2 * width)
        copies = [
            pltpu.make_async_copy(src.at[:, :, two], dst.at[:, :, two], load_sem.at[k, i])
            for i, (src, dst) in enumerate(((lp_hbm, cor), (base_hbm, basev), (err_hbm, errv)))
        ]
        for copy in copies:
            copy.start()
        loads.append(copies)

    load(0)
    barrier = pltpu.get_barrier_semaphore()

    def greet(replica, there):
        pl.semaphore_signal(barrier, inc=1, device_id={"replica": replica, "fsdp": there}, device_id_type=MESH)

    for k in range(1, replicas):
        greet(lax.rem(r + k, replicas), f)
    for k in range(1, nx):
        greet(2 * y + 1 - c, z * nx + lax.rem(x + k, nx))
    for k in range(1, fsdp):
        greet(r, lax.rem(f + k, fsdp))
    for k in range(1, chips):
        load(k)
    load_momentum = pltpu.make_async_copy(mom_hbm, momv, mom_sem.at[0])

    def correct(n):
        if n < chips:
            for copy in loads[n]:
                copy.wait()
        at_cols = cols(order[n])
        cor[:, :, at_cols] = basev[:, :, at_cols] - cor[:, :, at_cols] + errv[:, :, at_cols]

    for k in range(chips):
        write_start_factor(seed_ref[0], order[chips + k] * width, start.at[k])
        correct(k)
        if k == 0:
            pl.semaphore_wait(barrier, replicas - 1 + nx - 1 + fsdp - 1)
        send(cor.at[:, :, cols(order[k])], sib.at[k], p1_send.at[k], p1_recv.at[k], sibling)
    load_momentum.start()
    for k in range(chips):
        correct(chips + k)

    def paired(k):
        wait_for(sib.at[k], p1_recv.at[k])
        sib[k] = sib[k] + cor[:, :, cols(order[chips + k])]

    def hop(n, src, dst, shift):
        send(src, dst, p2_send.at[n], p2_recv.at[n], along_y(shift))
        drains.append((None, src, p2_send.at[n]))

    paired(0)
    hop(0, sib.at[0, 0], relay.at[0], 1)
    hop(1, sib.at[0, 1], relay.at[1], 3)

    scale = 3.4641016 / 65521.0 / 2.0 / replicas
    left_terms = times_start_factor(sib[0].reshape(rows, width), start[0])
    for k in range(1, chips):
        paired(k)
        if k == 1:
            hop(2, sib.at[1, 1], rs.at[0, 1], 1)
        if k == 2:
            hop(3, sib.at[2, 0], rs.at[1, 0], 3)
        left_terms = left_terms + times_start_factor(sib[k].reshape(rows, width), start[k])
    part[...] = (left_terms * scale).reshape(part.shape)
    parts[r] = part[c]
    for k in sorted(range(1, replicas), key=lambda k: -min(k, replicas - k)):
        to = lax.rem(r + k, replicas)
        send(part.at[lax.rem(to, 2)], parts.at[r], p3_sem.at[0], p3_sem.at[1], {"replica": to, "fsdp": f})
    drains.append((None, parts.at[pl.ds(0, replicas - 1)], p3_sem.at[0]))

    wait_for(relay.at[0], p2_recv.at[0])
    relay[0] = relay[0] + sib[1, 0]
    hop(4, relay.at[0], rs.at[0, 0], 1)
    wait_for(relay.at[1], p2_recv.at[1])
    relay[1] = relay[1] + sib[2, 1]
    hop(5, relay.at[1], rs.at[1, 1], 3)

    wait_for(parts.at[pl.ds(0, replicas - 1)], p3_sem.at[1])
    total = parts[0]
    for k in range(1, replicas):
        total = total + parts[k]
    line[z] = total

    has_tile, my_tile = tile_of(f, 2 * tiles, fsdp)
    owner = jnp.logical_and(has_tile, lax.rem(my_tile, 2) == c)
    other = jnp.logical_not(owner)
    my_tile = my_tile // 2

    def to_owner(t):
        to = owner_of(2 * t + c, 2 * tiles, fsdp)
        tile = blk.at[t]

        @pl.when(to != f)
        def _():
            send(tile, at.at[in_line(f)], p5_sem.at[0], p5_sem.at[1], {"replica": r, "fsdp": to})

        @pl.when(to == f)
        def _():
            at[in_line(f)] = tile[...]

    for k in sorted(range(1, nz), key=lambda k: -min(k, nz - k)):
        to = lax.rem(z + k, nz) * nx + x
        send(line.at[z], line.at[z], pz_sem.at[0], pz_sem.at[1], {"replica": r, "fsdp": to})
    drains.append((None, line.at[pl.ds(0, nz - 1)], pz_sem.at[0]))
    for n, (a, b) in zip((2, 3, 4, 5), ((0, 1), (1, 0), (0, 0), (1, 1)), strict=True):
        wait_for(rs.at[a, b], p2_recv.at[n])
    mean = (sib[3] + rs[0] + rs[1]) * (1.0 / replicas)
    for t in range(tiles):
        blk[t] = mean[:, :, t * LANES : (t + 1) * LANES]
    for t in range(tiles):
        to_owner(lax.rem(t + f * tiles // fsdp, tiles))
    wait_for(line.at[pl.ds(0, nz - 1)], pz_sem.at[1])
    for k in sorted(range(nx), key=lambda k: -min(k, nx - k)):
        there = z * nx + lax.rem(x + k, nx)
        has, tile = tile_of(there, 2 * tiles, fsdp)
        core = lax.rem(tile, 2)
        remote = has if k else jnp.logical_and(has, core != c)

        @pl.when(remote)
        def _():
            send(line, left.at[c * nx + x], px_send.at[k], px_recv.at[0], {"replica": 2 * y + core, "fsdp": there})

        drains.append((remote, line, px_send.at[k]))
    drains.append((owner, at.at[pl.ds(0, tiles - 1)], p5_sem.at[0]))
    drains.append((other, at.at[pl.ds(0, tiles)], p5_sem.at[0]))

    cut = tiles // 2
    sizes = (cut, tiles - cut)
    my_half = my_tile // cut
    my_tile = r * tiles + my_tile

    @pl.when(owner)
    def _():
        left[c * nx + x] = line[...]
        wait_for(left.at[pl.ds(0, 2 * nx - 1)], px_recv.at[0])
        whole = left[...].reshape(fsdp * rows, RANK)
        against = (((0,), (0,)), ((), ()))
        mg[...] = lax.dot_general(
            whole, whole, against, precision=HIGHEST, preferred_element_type=jnp.float32
        ).reshape(mg.shape)
        invert(mg)
        wait_for(at.at[pl.ds(0, fsdp - 1)], p5_sem.at[1])

        def left_half(h):
            return left[pl.ds(h * nx, nx)].reshape(fsdp * half, RANK)

        products = [
            lax.dot_general(
                left_half(h),
                at[:, h].reshape(fsdp * half, LANES),
                against,
                precision=HIGHEST,
                preferred_element_type=jnp.float32,
            )
            for h in range(2)
        ]
        weights = jnp.dot(
            mg[...].reshape(RANK, RANK),
            products[0] + products[1],
            precision=HIGHEST,
            preferred_element_type=jnp.float32,
        )
        for h in range(2):
            ap[:, h] = jnp.dot(
                left_half(h), weights, precision=HIGHEST, preferred_element_type=jnp.float32
            ).reshape(fsdp, half, LANES)

        def give(dz, dx):
            to = lax.rem(z + dz, nz) * nx + lax.rem(x + dx, nx)
            send(ap.at[in_line(to)], apx.at[my_tile], p7_send.at[0], p7_recv.at[my_half], {"replica": r, "fsdp": to})
            return 0

        for dz, dx in far_first:
            give(dz, dx)
        apx[my_tile] = ap[in_line(f)]

    def returned(h):
        mine_too = jnp.logical_and(owner, my_half == h)

        @pl.when(mine_too)
        def _():
            wait_for(apx.at[pl.ds(0, sizes[h] - 1)], p7_recv.at[h])

        @pl.when(jnp.logical_not(mine_too))
        def _():
            wait_for(apx.at[pl.ds(0, sizes[h])], p7_recv.at[h])

    drains.append((owner, ap.at[pl.ds(0, fsdp - 1)], p7_send.at[0]))
    def place(block, h):
        return apx.at[pl.ds(block * tiles + h * cut, sizes[h])]

    def end(block, h):
        for t in range(sizes[h]):
            tile = block * tiles + h * cut + t
            at_cols = pl.ds(pl.multiple_of(tile * LANES, LANES), LANES)
            out[:, :, at_cols] = apx[tile]

    def pass_on(h):
        for k, shift in enumerate(shifts[:-1]):
            send(place(r, h), place(r, h), p8_send.at[h, k], p8_recv.at[h, k], along_y(shift))
            drains.append((None, place(r, h), p8_send.at[h, k]))
        send(place(r, h), place(r, h), p9_send.at[h, chips - 1], p9_recv.at[h, chips - 1], sibling)
        drains.append((None, place(r, h), p9_send.at[h, chips - 1]))

    returned(0)
    pass_on(0)
    load_momentum.wait()
    for k in range(chips):
        wait_for(sib.at[k], p1_send.at[k])
    end(r, 0)
    returned(1)
    pass_on(1)
    end(r, 1)
    for h in range(2):
        for k in (1, 2, 0):
            block = 2 * chip(chips - shifts[k]) + c
            wait_for(place(block, h), p8_recv.at[h, k])
            send(place(block, h), place(block, h), p9_send.at[h, k], p9_recv.at[h, k], sibling)
            drains.append((None, place(block, h), p9_send.at[h, k]))
            end(block, h)
        for k in (3, 1, 2, 0):
            block = 2 * chip(chips - shifts[k]) + 1 - c
            wait_for(place(block, h), p9_recv.at[h, k])
            end(block, h)
    finish()


def on_device(local_params, outer_base, error_memory, momentum, start_seed):
    replicas, fsdp = lax.axis_size("replica"), lax.axis_size("fsdp")
    rows, columns = outer_base.shape
    half = rows // 2
    tiles = columns // replicas // LANES
    width = tiles * LANES
    chips = replicas // 2
    f32 = jnp.float32
    whole = (2, half, columns)
    dma = pltpu.SemaphoreType.DMA
    in_hbm = pl.BlockSpec(memory_space=pltpu.HBM)
    corrected, base, old_momentum, approx = pl.pallas_call(
        functools.partial(kernel, replicas, fsdp, tiles),
        out_shape=[pltpu.VMEM(whole, f32)] * 4,
        in_specs=[pl.BlockSpec(memory_space=pltpu.SMEM), in_hbm, in_hbm, in_hbm, in_hbm],
        out_specs=[pl.BlockSpec(memory_space=pltpu.VMEM)] * 4,
        scratch_shapes=[
            pltpu.VMEM(whole, f32),
            pltpu.VMEM((chips, 2, half, width), f32),
            pltpu.VMEM((2, half, width), f32),
            pltpu.VMEM((2, 2, half, width), f32),
            pltpu.VMEM((tiles, 2, half, LANES), f32),
            pltpu.VMEM((chips, width, 2 * RANK), jnp.bfloat16),
            pltpu.VMEM((2, half, RANK), f32),
            pltpu.VMEM((replicas, half, RANK), f32),
            pltpu.VMEM((fsdp // along_x(fsdp), half, RANK), f32),
            pltpu.VMEM((2 * along_x(fsdp), fsdp // along_x(fsdp), half, RANK), f32),
            pltpu.VMEM((fsdp, 2, half, LANES), f32),
            pltpu.VMEM((fsdp, 2, half, LANES), f32),
            pltpu.VMEM((columns // LANES, 2, half, LANES), f32),
            pltpu.VMEM((RANK // SUBS, SUBS, RANK), f32),
            dma((chips, 3)),
            dma((1,)),
            dma((chips,)),
            dma((chips,)),
            dma((6,)),
            dma((6,)),
            dma((2,)),
            dma((2,)),
            dma((4,)),
            dma((1,)),
            dma((2,)),
            dma((1,)),
            dma((2,)),
            dma((2, chips)),
            dma((2, chips)),
            dma((2, chips)),
            dma((2, chips)),
        ],
        compiler_params=pltpu.CompilerParams(
            collective_id=0, has_side_effects=True, vmem_limit_bytes=59 * 1024 * 1024
        ),
        cost_estimate=pl.CostEstimate(flops=10**9, bytes_accessed=4 * 10**6, transcendentals=0),
        name="approximate",
    )(
        start_seed,
        local_params.reshape(whole),
        outer_base.reshape(whole),
        error_memory.reshape(whole),
        momentum.reshape(whole),
    )
    new_error = corrected - approx
    new_momentum = 0.9 * old_momentum + approx
    new_base = base - 0.7 * (approx + 0.9 * new_momentum)
    return (new_error.reshape(1, rows, columns), new_base.reshape(rows, columns), new_momentum.reshape(rows, columns))


def solution(mesh):
    placed = (
        P("replica", "fsdp", None),
        P("fsdp", None),
        P("replica", "fsdp", None),
        P("fsdp", None),
        P(),
    )
    return jax.shard_map(
        on_device,
        mesh=mesh,
        in_specs=placed,
        out_specs=(P("replica", "fsdp", None), P("fsdp", None), P("fsdp", None)),
        check_vma=False,
    )
```

```python
import functools

import jax
import jax.numpy as jnp
from jax import lax
from jax.experimental import pallas as pl
from jax.experimental.pallas import tpu as pltpu
from jax.sharding import PartitionSpec as P

RANK = 128
LANES = 128
SUBS = 8
HIGHEST = lax.Precision.HIGHEST
MESH = pl.DeviceIdType.MESH


def owner_of(tile, tiles, fsdp):
    return tile if tiles == fsdp else tile + 1 + tile // 8


def tile_of(f, tiles, fsdp):
    if tiles == fsdp:
        return f >= 0, f
    tile = f - 1 - f // 9
    return jnp.logical_and(lax.rem(f, 9) != 0, tile < tiles), tile


def write_start_factor(seed, first_row, out_ref):
    two = 2 * SUBS
    k = lax.broadcasted_iota(jnp.int32, (two, LANES), 1)
    j = lax.broadcasted_iota(jnp.int32, (two, LANES), 0) + first_row
    mixed = lax.rem(181 * j + 359 * k + 1013 * seed, 65521)
    added = 7 * j + 3 * k

    def rows(i, carry):
        mixed, added = carry
        low = jnp.where(mixed >= 65498, mixed - 65498, jnp.where(mixed >= 32749, mixed - 32749, mixed))
        value = mixed * low + added
        quotient = (value.astype(jnp.float32) * ((1.0 - 2.0**-21) / 65521.0)).astype(jnp.int32)
        rest = value - quotient * 65521
        rest = jnp.where(rest >= 65521, rest - 65521, rest)
        odd = 2 * rest - 65521
        high = (odd + 256) >> 9
        here = pl.ds(pl.multiple_of(i * two, two), two)
        out_ref[here, :LANES] = high.astype(jnp.float32).astype(jnp.bfloat16)
        out_ref[here, LANES:] = (odd - 512 * high).astype(jnp.float32).astype(jnp.bfloat16)
        mixed = mixed + 181 * two
        return jnp.where(mixed >= 65521, mixed - 65521, mixed), added + 7 * two

    lax.fori_loop(0, out_ref.shape[0] // two, rows, (mixed, added), unroll=8)


def times_start_factor(x, start):
    parts, rest = [], x
    for _ in range(3):
        parts.append(rest.astype(jnp.bfloat16))
        rest = rest - parts[-1].astype(jnp.float32)
    both = jnp.dot(jnp.concatenate(parts, axis=0), start, preferred_element_type=jnp.float32)
    wide = 512.0 * both[:, :LANES] + both[:, LANES:]
    n = x.shape[0]
    return (wide[2 * n :] + wide[n : 2 * n]) + wide[:n]


def invert(m):
    sub = lax.broadcasted_iota(jnp.int32, (SUBS, LANES), 0)
    lane = lax.broadcasted_iota(jnp.int32, (SUBS, LANES), 1)

    def col(x, at):
        return jnp.broadcast_to(x[:, at : at + 1], (SUBS, LANES))

    def row(x, i):
        return jnp.broadcast_to(x[i : i + 1, :], (SUBS, LANES))

    panels = RANK // SUBS
    for p in range(panels):
        first = SUBS * p
        x = m[p]
        cols = [col(x, first + j) for j in range(SUBS)]
        inside = jnp.logical_and(lane >= first, lane < first + SUBS)
        x = jnp.where(inside, jnp.where(lane - first == sub, 1.0, 0.0), x)
        scales = jnp.ones_like(x)
        for i in range(SUBS):
            pivot = row(cols[i], i)
            scale = 1.0 / pivot
            scales = jnp.where(sub == i, scale, scales)
            by = jnp.where(sub == i, 0.0, cols[i])

            def step(x):
                return x - by * (row(x, i) * scale)

            x = step(x)
            for j in range(i + 1, SUBS):
                cols[j] = step(cols[j])
        x = x * scales
        rows = [row(x, j) for j in range(SUBS)]
        for q in [(p + 1 + k) % panels for k in range(panels - 1)]:
            a = m[q]
            t = [col(a, first + j) * rows[j] for j in range(SUBS)]
            taken = ((t[0] + t[1]) + (t[2] + t[3])) + ((t[4] + t[5]) + (t[6] + t[7]))
            m[q] = jnp.where(inside, 0.0, a) - taken
        m[p] = x


def along_x(fsdp):
    return 4 if fsdp % 8 == 0 else 2


def wait_for(ref, sem):
    if 0 in ref.shape:
        return
    pltpu.make_async_copy(ref, ref, sem).wait()


def kernel(
    replicas, fsdp, tiles,
    seed_ref, lp_hbm, base_hbm, err_hbm, mom_hbm, cor, basev, momv, out,
    errv, sib, relay, rs, blk, start, part, parts, line, left, at, ap, apx, mg,
    load_sem, mom_sem, p1_send, p1_recv, p2_send, p2_recv, p3_sem, pz_sem, px_send, px_recv, p5_sem, p7_send, p7_recv,
    p8_send, p8_recv, p9_send, p9_recv,
):
    chips = replicas // 2
    width = tiles * LANES
    half = blk.shape[2]
    rows = 2 * half
    r = lax.axis_index("replica")
    f = lax.axis_index("fsdp")
    c = lax.rem(r, 2)
    y = r // 2
    nx = along_x(fsdp)
    nz = fsdp // nx
    z, x = f // nx, lax.rem(f, nx)
    far_first = [
        (dz, dx)
        for dz in sorted(range(nz), key=lambda k: -min(k, nz - k))
        for dx in sorted(range(nx), key=lambda k: -min(k, nx - k))
        if dz or dx
    ]
    sibling = {"replica": 2 * y + 1 - c, "fsdp": f}
    shifts = [2, 1, 3, 0]

    def cols(block):
        return pl.ds(pl.multiple_of(block * width, LANES), width)

    def chip(shift):
        return lax.rem(y + shift, chips)

    def along_y(shift):
        return {"replica": 2 * chip(shift) + c, "fsdp": f}

    def send(src, dst, s, d, to):
        pltpu.make_async_remote_copy(
            src_ref=src, dst_ref=dst, send_sem=s, recv_sem=d, device_id=to, device_id_type=MESH
        ).start()

    drains = []

    def finish():
        for condition, ref, sem in drains:
            if condition is None:
                wait_for(ref, sem)
            else:

                @pl.when(condition)
                def _():
                    wait_for(ref, sem)

    def in_line(f):
        return lax.rem(f, nx) * nz + f // nx

    order = [2 * chip(s) + 1 - c for s in shifts] + [2 * chip(s) + c for s in shifts]
    loads = []

    def load(k):
        two = pl.ds(pl.multiple_of(chip(shifts[k]) * 2 * width, LANES), 2 * width)
        copies = [
            pltpu.make_async_copy(src.at[:, :, two], dst.at[:, :, two], load_sem.at[k, i])
            for i, (src, dst) in enumerate(((lp_hbm, cor), (base_hbm, basev), (err_hbm, errv)))
        ]
        for copy in copies:
            copy.start()
        loads.append(copies)

    for k in range(chips):
        load(k)
    barrier = pltpu.get_barrier_semaphore()

    def greet(replica, there):
        pl.semaphore_signal(barrier, inc=1, device_id={"replica": replica, "fsdp": there}, device_id_type=MESH)

    for k in range(1, replicas):
        greet(lax.rem(r + k, replicas), f)
    for k in range(1, nx):
        greet(2 * y + 1 - c, z * nx + lax.rem(x + k, nx))
    for k in range(1, fsdp):
        greet(r, lax.rem(f + k, fsdp))
    load_momentum = pltpu.make_async_copy(mom_hbm, momv, mom_sem.at[0])

    def correct(n):
        if n < chips:
            for copy in loads[n]:
                copy.wait()
        at_cols = cols(order[n])
        cor[:, :, at_cols] = basev[:, :, at_cols] - cor[:, :, at_cols] + errv[:, :, at_cols]

    for k in range(chips):
        write_start_factor(seed_ref[0], order[chips + k] * width, start.at[k])
        correct(k)
        if k == 0:
            pl.semaphore_wait(barrier, replicas - 1 + nx - 1 + fsdp - 1)
        send(cor.at[:, :, cols(order[k])], sib.at[k], p1_send.at[k], p1_recv.at[k], sibling)
    load_momentum.start()
    for k in range(chips):
        correct(chips + k)

    def paired(k):
        wait_for(sib.at[k], p1_recv.at[k])
        sib[k] = sib[k] + cor[:, :, cols(order[chips + k])]

    def hop(n, src, dst, shift):
        send(src, dst, p2_send.at[n], p2_recv.at[n], along_y(shift))
        drains.append((None, src, p2_send.at[n]))

    paired(0)
    hop(0, sib.at[0, 0], relay.at[0], 1)
    hop(1, sib.at[0, 1], relay.at[1], 3)

    scale = 3.4641016 / 65521.0 / 2.0 / replicas
    left_terms = times_start_factor(sib[0].reshape(rows, width), start[0])
    for k in range(1, chips):
        paired(k)
        if k == 1:
            hop(2, sib.at[1, 1], rs.at[0, 1], 1)
        if k == 2:
            hop(3, sib.at[2, 0], rs.at[1, 0], 3)
        left_terms = left_terms + times_start_factor(sib[k].reshape(rows, width), start[k])
    part[...] = (left_terms * scale).reshape(part.shape)
    parts[r] = part[c]
    for k in sorted(range(1, replicas), key=lambda k: -min(k, replicas - k)):
        to = lax.rem(r + k, replicas)
        send(part.at[lax.rem(to, 2)], parts.at[r], p3_sem.at[0], p3_sem.at[1], {"replica": to, "fsdp": f})
    drains.append((None, parts.at[pl.ds(0, replicas - 1)], p3_sem.at[0]))

    wait_for(relay.at[0], p2_recv.at[0])
    relay[0] = relay[0] + sib[1, 0]
    hop(4, relay.at[0], rs.at[0, 0], 1)
    wait_for(relay.at[1], p2_recv.at[1])
    relay[1] = relay[1] + sib[2, 1]
    hop(5, relay.at[1], rs.at[1, 1], 3)

    wait_for(parts.at[pl.ds(0, replicas - 1)], p3_sem.at[1])
    total = parts[0]
    for k in range(1, replicas):
        total = total + parts[k]
    line[z] = total

    has_tile, my_tile = tile_of(f, 2 * tiles, fsdp)
    owner = jnp.logical_and(has_tile, lax.rem(my_tile, 2) == c)
    other = jnp.logical_not(owner)
    my_tile = my_tile // 2

    def to_owner(t):
        to = owner_of(2 * t + c, 2 * tiles, fsdp)
        tile = blk.at[t]

        @pl.when(to != f)
        def _():
            send(tile, at.at[in_line(f)], p5_sem.at[0], p5_sem.at[1], {"replica": r, "fsdp": to})

        @pl.when(to == f)
        def _():
            at[in_line(f)] = tile[...]

    for k in sorted(range(1, nz), key=lambda k: -min(k, nz - k)):
        to = lax.rem(z + k, nz) * nx + x
        send(line.at[z], line.at[z], pz_sem.at[0], pz_sem.at[1], {"replica": r, "fsdp": to})
    drains.append((None, line.at[pl.ds(0, nz - 1)], pz_sem.at[0]))
    for n, (a, b) in zip((2, 3, 4, 5), ((0, 1), (1, 0), (0, 0), (1, 1)), strict=True):
        wait_for(rs.at[a, b], p2_recv.at[n])
    mean = (sib[3] + rs[0] + rs[1]) * (1.0 / replicas)
    for t in range(tiles):
        blk[t] = mean[:, :, t * LANES : (t + 1) * LANES]
    for t in range(tiles):
        to_owner(lax.rem(t + f * tiles // fsdp, tiles))
    wait_for(line.at[pl.ds(0, nz - 1)], pz_sem.at[1])
    for k in sorted(range(nx), key=lambda k: -min(k, nx - k)):
        there = z * nx + lax.rem(x + k, nx)
        has, tile = tile_of(there, 2 * tiles, fsdp)
        core = lax.rem(tile, 2)
        remote = has if k else jnp.logical_and(has, core != c)

        @pl.when(remote)
        def _():
            send(line, left.at[c * nx + x], px_send.at[k], px_recv.at[0], {"replica": 2 * y + core, "fsdp": there})

        drains.append((remote, line, px_send.at[k]))
    drains.append((owner, at.at[pl.ds(0, tiles - 1)], p5_sem.at[0]))
    drains.append((other, at.at[pl.ds(0, tiles)], p5_sem.at[0]))

    cut = tiles // 2
    sizes = (cut, tiles - cut)
    my_half = my_tile // cut
    my_tile = r * tiles + my_tile

    @pl.when(owner)
    def _():
        left[c * nx + x] = line[...]
        wait_for(left.at[pl.ds(0, 2 * nx - 1)], px_recv.at[0])
        whole = left[...].reshape(fsdp * rows, RANK)
        against = (((0,), (0,)), ((), ()))
        mg[...] = lax.dot_general(
            whole, whole, against, precision=HIGHEST, preferred_element_type=jnp.float32
        ).reshape(mg.shape)
        invert(mg)
        wait_for(at.at[pl.ds(0, fsdp - 1)], p5_sem.at[1])

        def left_half(h):
            return left[pl.ds(h * nx, nx)].reshape(fsdp * half, RANK)

        products = [
            lax.dot_general(
                left_half(h),
                at[:, h].reshape(fsdp * half, LANES),
                against,
                precision=HIGHEST,
                preferred_element_type=jnp.float32,
            )
            for h in range(2)
        ]
        weights = jnp.dot(
            mg[...].reshape(RANK, RANK),
            products[0] + products[1],
            precision=HIGHEST,
            preferred_element_type=jnp.float32,
        )
        for h in range(2):
            ap[:, h] = jnp.dot(
                left_half(h), weights, precision=HIGHEST, preferred_element_type=jnp.float32
            ).reshape(fsdp, half, LANES)

        def give(dz, dx):
            to = lax.rem(z + dz, nz) * nx + lax.rem(x + dx, nx)
            send(ap.at[in_line(to)], apx.at[my_tile], p7_send.at[0], p7_recv.at[my_half], {"replica": r, "fsdp": to})
            return 0

        for dz, dx in far_first:
            give(dz, dx)
        apx[my_tile] = ap[in_line(f)]

    def returned(h):
        mine_too = jnp.logical_and(owner, my_half == h)

        @pl.when(mine_too)
        def _():
            wait_for(apx.at[pl.ds(0, sizes[h] - 1)], p7_recv.at[h])

        @pl.when(jnp.logical_not(mine_too))
        def _():
            wait_for(apx.at[pl.ds(0, sizes[h])], p7_recv.at[h])

    drains.append((owner, ap.at[pl.ds(0, fsdp - 1)], p7_send.at[0]))
    def place(block, h):
        return apx.at[pl.ds(block * tiles + h * cut, sizes[h])]

    def end(block, h):
        for t in range(sizes[h]):
            tile = block * tiles + h * cut + t
            at_cols = pl.ds(pl.multiple_of(tile * LANES, LANES), LANES)
            out[:, :, at_cols] = apx[tile]

    def pass_on(h):
        for k, shift in enumerate(shifts[:-1]):
            send(place(r, h), place(r, h), p8_send.at[h, k], p8_recv.at[h, k], along_y(shift))
            drains.append((None, place(r, h), p8_send.at[h, k]))
        send(place(r, h), place(r, h), p9_send.at[h, chips - 1], p9_recv.at[h, chips - 1], sibling)
        drains.append((None, place(r, h), p9_send.at[h, chips - 1]))

    returned(0)
    pass_on(0)
    load_momentum.wait()
    for k in range(chips):
        wait_for(sib.at[k], p1_send.at[k])
    end(r, 0)
    returned(1)
    pass_on(1)
    end(r, 1)
    for h in range(2):
        for k in (1, 2, 0):
            block = 2 * chip(chips - shifts[k]) + c
            wait_for(place(block, h), p8_recv.at[h, k])
            send(place(block, h), place(block, h), p9_send.at[h, k], p9_recv.at[h, k], sibling)
            drains.append((None, place(block, h), p9_send.at[h, k]))
            end(block, h)
        for k in (3, 1, 2, 0):
            block = 2 * chip(chips - shifts[k]) + 1 - c
            wait_for(place(block, h), p9_recv.at[h, k])
            end(block, h)
    finish()


def on_device(local_params, outer_base, error_memory, momentum, start_seed):
    replicas, fsdp = lax.axis_size("replica"), lax.axis_size("fsdp")
    rows, columns = outer_base.shape
    half = rows // 2
    tiles = columns // replicas // LANES
    width = tiles * LANES
    chips = replicas // 2
    f32 = jnp.float32
    whole = (2, half, columns)
    dma = pltpu.SemaphoreType.DMA
    in_hbm = pl.BlockSpec(memory_space=pltpu.HBM)
    corrected, base, old_momentum, approx = pl.pallas_call(
        functools.partial(kernel, replicas, fsdp, tiles),
        out_shape=[pltpu.VMEM(whole, f32)] * 4,
        in_specs=[pl.BlockSpec(memory_space=pltpu.SMEM), in_hbm, in_hbm, in_hbm, in_hbm],
        out_specs=[pl.BlockSpec(memory_space=pltpu.VMEM)] * 4,
        scratch_shapes=[
            pltpu.VMEM(whole, f32),
            pltpu.VMEM((chips, 2, half, width), f32),
            pltpu.VMEM((2, half, width), f32),
            pltpu.VMEM((2, 2, half, width), f32),
            pltpu.VMEM((tiles, 2, half, LANES), f32),
            pltpu.VMEM((chips, width, 2 * RANK), jnp.bfloat16),
            pltpu.VMEM((2, half, RANK), f32),
            pltpu.VMEM((replicas, half, RANK), f32),
            pltpu.VMEM((fsdp // along_x(fsdp), half, RANK), f32),
            pltpu.VMEM((2 * along_x(fsdp), fsdp // along_x(fsdp), half, RANK), f32),
            pltpu.VMEM((fsdp, 2, half, LANES), f32),
            pltpu.VMEM((fsdp, 2, half, LANES), f32),
            pltpu.VMEM((columns // LANES, 2, half, LANES), f32),
            pltpu.VMEM((RANK // SUBS, SUBS, RANK), f32),
            dma((chips, 3)),
            dma((1,)),
            dma((chips,)),
            dma((chips,)),
            dma((6,)),
            dma((6,)),
            dma((2,)),
            dma((2,)),
            dma((4,)),
            dma((1,)),
            dma((2,)),
            dma((1,)),
            dma((2,)),
            dma((2, chips)),
            dma((2, chips)),
            dma((2, chips)),
            dma((2, chips)),
        ],
        compiler_params=pltpu.CompilerParams(
            collective_id=0, has_side_effects=True, vmem_limit_bytes=59 * 1024 * 1024
        ),
        cost_estimate=pl.CostEstimate(flops=10**9, bytes_accessed=4 * 10**6, transcendentals=0),
        name="approximate",
    )(
        start_seed,
        local_params.reshape(whole),
        outer_base.reshape(whole),
        error_memory.reshape(whole),
        momentum.reshape(whole),
    )
    new_error = corrected - approx
    new_momentum = 0.9 * old_momentum + approx
    new_base = base - 0.7 * (approx + 0.9 * new_momentum)
    return (new_error.reshape(1, rows, columns), new_base.reshape(rows, columns), new_momentum.reshape(rows, columns))


def solution(mesh):
    placed = (
        P("replica", "fsdp", None),
        P("fsdp", None),
        P("replica", "fsdp", None),
        P("fsdp", None),
        P(),
    )
    return jax.shard_map(
        on_device,
        mesh=mesh,
        in_specs=placed,
        out_specs=(P("replica", "fsdp", None), P("fsdp", None), P("fsdp", None)),
        check_vma=False,
    )
```
